512 devices in a mesh: row: 64 (over z, y), rep: 8 (over x, core).
Axes of the slice: x: 4, y: 8, z: 8, core: 2. Of those that a mesh axis runs over, the one named last changes fastest.
Arguments:
- features: bfloat16 [32768, 128], P('row'), may hold values from -6 to 6
- edge_tiles: bfloat16 [8192, 128, 128], P(('row', 'rep')), may hold values from -0.09375 to 0.09375
- tile_owner: int32 [8192, 1], P(('row', 'rep')), may hold values from 0 to 63; in each aligned block of 16 rows (0 to 15, 16 to 31, ...) at most 2 rows name the same one
- tile_block: int32 [8192], P(('row', 'rep')), may hold values from 0 to 3
- tile_row: int32 [8192], P(('row', 'rep')), may hold values from 0 to 3
- w_self: bfloat16 [128, 256], replicated, may hold values from -0.5 to 0.5
- w_neigh: bfloat16 [128, 256], replicated, may hold values from -0.5 to 0.5
- bias_vector: float32 [256], replicated, may hold values from -3 to 3
- cotangent: bfloat16 [32768, 256], P(('row', 'rep')), may hold values from -6 to 6
Outputs:
- hidden: bfloat16 [32768, 256], P(('row', 'rep'))
- grad_features: float32 [32768, 128], P(('row', 'rep'))
- grad_self: float32 [128, 256], replicated
- grad_neigh: float32 [128, 256], replicated
- grad_bias: float32 [256], replicated
The draws below stay inside these ranges and needn't reach their ends.
Inputs may be any that keep to these rules, and one draw needn't show every extreme that they name: `tile_owner`: among the 16 tiles of one device, no value occurs more than 2 times, and some value occurs exactly 2 times.
All inputs are finite; a program needn't handle non-finite values.
Results may differ from the reference program's by a relative error of at most 0.014.
Values may be sent and summed in bfloat16 or wider, within the bound.
A program may use at most 64 MiB of HBM per device.

```python
import math
import jax
import jax.numpy as jnp
import numpy as np
from jax import lax

F = 128
HID = 256
BLK = 128
NBD = 4
TPD = 16
CAP = 2
NODES = 32768
NBLK = 256
TILES = 8192
N_ROW = 64
N_REP = 8


def touch_ends(values, own_key, low, high):
    spot = [jax.random.randint(jax.random.fold_in(own_key, axis), (), 0, length) for axis, length in enumerate(values.shape)]
    longest = values.shape.index(max(values.shape))
    beside = spot[:longest] + [(spot[longest] + 1) % values.shape[longest]] + spot[longest + 1:]
    return values.at[tuple(spot)].set(low).at[tuple(beside)].set(high)


def level_of(stream_key, dims, cuts, low, high):
    gain = 1.0
    for axis_at, shards_of in cuts:
        steps = jax.random.uniform(jax.random.fold_in(jax.random.fold_in(stream_key, 6), axis_at), (shards_of,), jnp.float32, low / len(cuts), high / len(cuts))
        gain = gain * jnp.repeat(jnp.exp(steps), dims[axis_at] // shards_of).reshape((-1,) + (1,) * (len(dims) - 1 - axis_at))
    return gain


def shared_out(rng, own, number, rows, count, top, limit, slope):
    ranking = jax.random.permutation(rng, count)
    crowded, usual = portions_of(count, rows * top, limit, slope, True), portions_of(count, rows * top, limit, slope, False)
    places = jnp.arange(count)

    def named(sizes, offset_by):
        used = int((sizes > 0).sum())
        fixed = max(1, used // 4)
        moved = fixed + (places - fixed + offset_by * (used - fixed)) % max(1, count - fixed)
        return jnp.zeros((count,), jnp.int32).at[ranking[jnp.where(places < fixed, places, moved)]].set(jnp.asarray(sizes, jnp.int32))

    sizes = jnp.where(number % 4 == 0, named(crowded, number // 4), named(usual, number - number // 4 - 1))
    mixed = jax.random.permutation(jax.random.fold_in(own, 3), count)
    source_of, receiver = mixed[0:count // 2 * 2:2], mixed[1:count // 2 * 2:2]
    margin = jnp.minimum(sizes[source_of] - 1, limit - sizes[receiver]) // 2
    margin = jnp.where((source_of == ranking[0]) | (receiver == ranking[0]) | (sizes[receiver] == 0), 0, jnp.maximum(margin, 0))
    moved = jax.random.randint(jax.random.fold_in(own, 4), (count // 2,), 0, 1 << 20) % (margin + 1)
    sizes = sizes.at[source_of].add(-moved).at[receiver].add(moved)
    labels = jnp.searchsorted(jnp.cumsum(sizes), jnp.arange(rows * top), side="right").astype(jnp.int32)
    listing = labels.reshape(top, rows).T
    listing = listing[jax.random.permutation(jax.random.fold_in(own, 1), rows)]
    offset_by = jax.random.randint(jax.random.fold_in(own, 2), (rows, 1), 0, top)
    return jnp.take_along_axis(listing, (jnp.arange(top)[None, :] + offset_by) % top, axis=1)


def portions_of(number_of, total, most, slope, full):
    weights = [(1 << 20) // math.isqrt(grade ** slope) + 1 for grade in range(1, number_of + 1)]
    largest = most if full else min(most, max(-(-total // number_of), total * weights[0] // sum(weights)))
    least = 1 if total - largest >= number_of - 1 else 0
    counts, surplus = [largest] + [least] * (number_of - 1), total - largest - least * (number_of - 1)
    while surplus > 0:
        candidates = [i for i in range(1, number_of) if counts[i] < largest] or [i for i in range(1, number_of) if counts[i] < most]
        mass, budget = sum([weights[i] for i in candidates]), surplus
        for i in candidates:
            more = min(most - counts[i], max(1, budget * weights[i] // mass), surplus)
            counts[i] = counts[i] + more
            surplus = surplus - more
    return np.array(counts)


def bell_draw(key, dims, width, reach, split=(), held_as=jnp.bfloat16):
    entries = jax.random.normal(key, dims, jnp.float32) * width
    if len(split) > 0:
        entries = level_of(key, dims, split, -0.22, 0.18) * entries
    return jnp.clip(entries, min=-reach, max=reach).astype(held_as)


def setup_inputs(seed: int = 0) -> dict:
    seeds = jax.random.split(jax.random.key(seed), 10)
    features = bell_draw(seeds[0], (NODES, F), 1.0, 6.0, ((0, 64),))
    edge_tiles = bell_draw(seeds[1], (TILES, BLK, BLK), (N_REP * TPD * BLK // NBD) ** -0.5, 0.09375, ((0, 512),))
    tile_owner_keys = jax.random.split(jax.random.fold_in(seeds[2], 1), TILES // TPD)
    tile_owner_turns = jax.random.permutation(jax.random.fold_in(seeds[2], 3), TILES // TPD)
    tile_owner = jax.vmap(lambda own, number: shared_out(jax.random.fold_in(seeds[2], 2), own, number, TPD, N_ROW, 1, CAP, 2))(tile_owner_keys, tile_owner_turns).reshape((TILES, 1))
    tile_block = touch_ends(jax.random.randint(seeds[3], (TILES,), 0, NBD), jax.random.fold_in(seeds[3], 1), 0, NBD - 1).astype(jnp.int32)
    tile_row = touch_ends(jax.random.randint(seeds[4], (TILES,), 0, NBD), jax.random.fold_in(seeds[4], 1), 0, NBD - 1).astype(jnp.int32)
    w_self = bell_draw(seeds[5], (F, HID), F ** -0.5, 0.5)
    w_neigh = bell_draw(seeds[6], (F, HID), F ** -0.5, 0.5)
    bias_vector = bell_draw(seeds[7], (HID,), 0.5, 3.0, (), jnp.float32)
    cotangent = bell_draw(seeds[8], (NODES, HID), 1.0, 6.0, ((0, 512),))
    return {"features": features, "edge_tiles": edge_tiles, "tile_owner": tile_owner, "tile_block": tile_block, "tile_row": tile_row, "w_self": w_self, "w_neigh": w_neigh, "bias_vector": bias_vector, "cotangent": cotangent}


def reference(features, edge_tiles, tile_owner, tile_block, tile_row, w_self, w_neigh, bias_vector, cotangent):
    groups = N_ROW * N_REP
    highest = lax.Precision.HIGHEST
    feature_blocks = features.reshape(NBLK, BLK, F)
    tile_groups = edge_tiles.reshape(groups, TPD, BLK, BLK)
    column_blocks = (tile_owner[:, 0].astype(jnp.int32) * NBD + tile_block.astype(jnp.int32)).reshape(groups, TPD)
    device_rows = (jnp.arange(TILES, dtype=jnp.int32) // (TPD * N_REP)) * NBD
    row_blocks = (device_rows + tile_row.astype(jnp.int32)).reshape(groups, TPD)

    def forward_step(total, item):
        tiles_here, columns, rows = item
        product = jnp.einsum("tij,tjf->tif", tiles_here.astype(jnp.float32),
                             feature_blocks[columns].astype(jnp.float32), precision=highest)
        return total.at[rows].add(product), None

    aggregate, _ = lax.scan(forward_step, jnp.zeros((NBLK, BLK, F), jnp.float32),
                            (tile_groups, column_blocks, row_blocks))
    aggregate_b = aggregate.reshape(NODES, F).astype(jnp.bfloat16)
    preact = (jnp.dot(features, w_self, preferred_element_type=jnp.float32)
              + jnp.dot(aggregate_b, w_neigh, preferred_element_type=jnp.float32) + bias_vector)
    hidden = jax.nn.silu(preact).astype(jnp.bfloat16)
    sigmoid_part = jax.nn.sigmoid(preact)
    dpre = cotangent.astype(jnp.float32) * sigmoid_part * (1.0 + preact * (1.0 - sigmoid_part))
    dpre_b = dpre.astype(jnp.bfloat16)
    scale = float(NODES) ** -0.5
    grad_self = jnp.dot(features.T, dpre_b, preferred_element_type=jnp.float32) * scale
    grad_neigh = jnp.dot(aggregate_b.T, dpre_b, preferred_element_type=jnp.float32) * scale
    grad_bias = jnp.sum(dpre, axis=0) * scale
    dagg = jnp.dot(dpre_b, w_neigh.T, preferred_element_type=jnp.float32).astype(jnp.bfloat16)
    dagg_blocks = dagg.reshape(NBLK, BLK, F)

    def backward_step(total, item):
        tiles_here, columns, rows = item
        product = jnp.einsum("tij,tif->tjf", tiles_here.astype(jnp.float32),
                             dagg_blocks[rows].astype(jnp.float32), precision=highest)
        rounded = lax.optimization_barrier(product.astype(jnp.bfloat16))
        return total.at[columns].add(rounded.astype(jnp.float32)), None

    back, _ = lax.scan(backward_step, jnp.zeros((NBLK, BLK, F), jnp.float32),
                       (tile_groups, column_blocks, row_blocks))
    grad_features = jnp.dot(dpre_b, w_self.T, preferred_element_type=jnp.float32) + back.reshape(NODES, F)
    return hidden, grad_features, grad_self, grad_neigh, grad_bias
```

```python
import jax
import jax.numpy as jnp
from jax import lax
from jax.experimental import pallas as pl
from jax.experimental.pallas import tpu as pltpu
from jax.sharding import PartitionSpec as P

MESH = pl.DeviceIdType.MESH
BF = jnp.bfloat16
F32 = jnp.float32


def swap_matrix(first, second):
    size = first * second
    out = lax.broadcasted_iota(jnp.int32, (size, size), 0)
    src = lax.broadcasted_iota(jnp.int32, (size, size), 1)
    match = (out // first == src % second) & (out % first == src // second)
    return match.astype(F32).astype(BF)


def dot(a, b):
    return jnp.dot(a, b, preferred_element_type=F32)


def make_kernel(nz, ny, nrep, tpd, blk, width, hid, nbd):
    cs = blk // nrep
    nodes = nbd * blk
    share = nodes // nrep
    half = nbd // 2
    npos = nbd * nz * ny
    hpos = npos // 2
    tiles_all = nrep * tpd
    scale = float(nz * ny * nodes) ** -0.5
    assert nz == ny and hid == 2 * width
    wrows = 4 * width // nrep
    yrows = wrows // ny

    def kernel(
        feat, tiles, owner, tblock, trow, w_self, w_neigh, bias, cot,
        hid_o, gf_o, gs_o, gn_o, gb_o,
        meta_s, meta, xt, ysend, tt, f1, f2, ttm, fg, a0, a1, dense, dg0, dg, o0, b1, b2s, b2,
        r0, r1, gl, g1, g2s, g2, g3s, g3, g4, g5, send, recv,
    ):
        row = lax.axis_index("row")
        p = lax.axis_index("rep")
        z = row // ny
        y = row - z * ny

        def on_rep(q):
            return (row, q)

        def on_z(q):
            return (q * ny + y, p)

        def on_y(q):
            return (z * ny + q, p)

        axes = ((nrep, p, on_rep), (nz, z, on_z), (ny, y, on_y))
        rep_axis, z_axis, y_axis = axes

        def others(axis):
            n, me, dev = axis
            order = []
            for d in range(1, n // 2 + 1):
                order.append(d)
                if n - d != d:
                    order.append(n - d)
            return [lax.rem(me + d, n) for d in order]

        def send_to(axis, t, src, dst, sem, left=None):
            pltpu.make_async_remote_copy(
                src_ref=src, dst_ref=dst, recv_sem=recv.at[sem],
                send_sem=send.at[sem if left is None else left],
                device_id=axis[2](t), device_id_type=MESH,
            ).start()

        def wait_bytes(ref, sem):
            pltpu.make_async_copy(ref, ref, sem).wait()

        def most(buf, n):
            return buf.at[pl.ds(0, n - 1)]

        barrier = pltpu.get_barrier_semaphore()
        count = 0
        for axis in axes:
            for t in others(axis):
                pl.semaphore_signal(barrier, inc=1, device_id=axis[2](t), device_id_type=MESH)
                count += 1

        lane = lax.broadcasted_iota(jnp.int32, (8, tiles_all), 1)
        code = jnp.zeros((8, tiles_all), jnp.int32)
        for k in range(tpd):
            own = owner[k, 0]
            own_z = own // ny
            own_y = own - own_z * ny
            b = tblock[k]
            low = b - (b // half) * half
            first = own_y * (2 * nz) + own_z * half + low
            second = hpos + own_z * (2 * ny) + own_y * half + low
            where_to = jnp.where(b < half, first, second) + trow[k] * npos
            code = jnp.where(lane == p * tpd + k, where_to, code)
        meta_s[...] = code

        pl.semaphore_wait(barrier, count)

        start = pl.multiple_of(p * cs, cs)
        f1[0, z] = feat[pl.ds(0, half), pl.ds(start, cs), :]
        f1[1, y] = feat[pl.ds(half, half), pl.ds(start, cs), :]
        for h, axis in ((0, z_axis), (1, y_axis)):
            for t in others(axis):
                send_to(axis, t, feat.at[pl.ds(h * half, half), pl.ds(start, cs), :],
                        f1.at[h, axis[1]], 2 + h)
        for t in others(rep_axis):
            send_to(rep_axis, t, meta_s, meta.at[p], 0)
        meta[p] = code

        for k in range(tpd):
            xt[k] = tiles[k].T
        tile_swap = swap_matrix(tpd, cs)
        node_swap = swap_matrix(nz * half, cs)

        def columns_of(t):
            part = xt[:, pl.ds(pl.multiple_of(t * cs, cs), cs), :].reshape(tpd * cs, blk)
            return dot(tile_swap, part).astype(BF).reshape(cs, tpd, blk)

        for t in others(rep_axis):
            ysend[t] = columns_of(t)
            send_to(rep_axis, t, ysend.at[t], tt.at[p], 1)
        tt[p] = columns_of(p)

        for h, axis in ((0, y_axis), (1, z_axis)):
            wait_bytes(most(f1.at[h], nz), recv.at[2 + h])
            part = dot(node_swap, f1[h].reshape(hpos // ny * cs, width)).astype(BF)
            f2[h, axis[1]] = part.reshape(cs, nz * half, width)
            for t in others(axis):
                send_to(axis, t, f2.at[h, axis[1]], f2.at[h, axis[1]], 4 + h)

        wait_bytes(most(meta, nrep), recv.at[0])
        codes = meta[0]
        for q in range(1, nrep):
            codes = codes + meta[q]
        codes = codes[0:1, :]
        rows_of = codes // npos
        pos = codes - rows_of * npos
        wait_bytes(most(tt, nrep), recv.at[1])
        for c in range(cs):
            turned = tt[:, c].reshape(tiles_all, blk).T
            for n in range(nbd):
                ttm[n * blk:(n + 1) * blk, c * tiles_all:(c + 1) * tiles_all] = jnp.where(
                    rows_of == n, turned, jnp.zeros_like(turned))
        pos_iota = lax.broadcasted_iota(jnp.int32, (npos, tiles_all), 0)
        select = (pos_iota == pos).astype(F32).T.astype(BF)

        for h in range(2):
            wait_bytes(most(f2.at[h], ny), recv.at[4 + h])
        for c in range(cs):
            here = jnp.concatenate(
                [f2[0, :, c].reshape(hpos, width), f2[1, :, c].reshape(hpos, width)], axis=0)
            fg[c * tiles_all:(c + 1) * tiles_all, :] = dot(select, here).astype(BF)
        partial = dot(ttm[...], fg[...]).astype(BF).reshape(nrep, share, width)
        a0[...] = partial
        for t in others(rep_axis):
            send_to(rep_axis, t, a0.at[t], a1.at[p], 6)
        a1[p] = a0[p]

        spread = jnp.concatenate(
            [(pos_iota + n * npos == codes).astype(F32).astype(BF) for n in range(nbd)], axis=0)
        for c in range(cs):
            placed = dot(spread, tt[:, c].reshape(tiles_all, blk)).astype(BF)
            for n in range(nbd):
                dense[c, :, n * blk:(n + 1) * blk] = placed[n * npos:(n + 1) * npos]

        per_block = blk // share if share < blk else 1
        if share < blk:
            which = p // per_block
            inside = pl.multiple_of((p - which * per_block) * share, share)
            own = feat[which, pl.ds(inside, share), :]
        else:
            own = feat[pl.ds(p * (share // blk), share // blk)].reshape(share, width)
        own_part = dot(own, w_self[...]) + bias[...]

        wait_bytes(most(a1, nrep), recv.at[6])
        total = a1[0].astype(F32)
        for q in range(1, nrep):
            total = total + a1[q].astype(F32)
        agg = total.astype(BF)
        pre = own_part + dot(agg, w_neigh[...])
        sig = jax.nn.sigmoid(pre)
        dpre = cot[...].astype(F32) * sig * (1.0 + pre * (1.0 - sig))
        dpre_b = dpre.astype(BF)
        contract_cols = (((1,), (1,)), ((), ()))
        dagg = lax.dot_general(dpre_b, w_neigh[...], contract_cols, preferred_element_type=F32)
        dg0[...] = dagg.astype(BF)
        for t in others(rep_axis):
            send_to(rep_axis, t, dg0, dg.at[p], 7)
        dg[p] = dg0[...]
        hid_o[...] = (pre * sig).astype(BF)

        contract_rows = (((0,), (0,)), ((), ()))
        bsum = jnp.sum(dpre, axis=0, keepdims=True)
        row8 = lax.broadcasted_iota(jnp.int32, (8, width), 0)
        bias_rows = jnp.where(row8 == 0, bsum[:, :width],
                              jnp.where(row8 == 1, bsum[:, width:], 0.0))
        both = jnp.concatenate([own, agg], axis=1)
        grads = lax.dot_general(both, dpre_b, contract_rows, preferred_element_type=F32)
        pieces = jnp.concatenate(
            [grads[w * width:(w + 1) * width, s * width:(s + 1) * width]
             for w in range(2) for s in range(2)], axis=0)
        for q in range(nrep):
            gl[q, 0:wrows, :] = pieces[q * wrows:(q + 1) * wrows]
            gl[q, wrows:wrows + 8, :] = bias_rows
        for t in others(rep_axis):
            send_to(rep_axis, t, gl.at[t], g1.at[p], 13)
        g1[p] = gl[p]

        wait_bytes(most(dg, nrep), recv.at[7])
        dall = dg[...].reshape(nodes, width)
        for c in range(cs):
            made = dot(dense[c], dall).astype(BF)
            o0[0, :, c] = made[:hpos].reshape(ny, nz * half, width)
            o0[1, :, c] = made[hpos:].reshape(nz, ny * half, width)
        for h, axis in ((0, y_axis), (1, z_axis)):
            for t in others(axis):
                send_to(axis, t, o0.at[h, t], b1.at[h, axis[1]], 8 + h)
            b1[h, axis[1]] = o0[h, axis[1]]

        def summed(buf, n):
            acc = buf[0]
            for q in range(1, n):
                acc = acc + buf[q]
            return acc

        wait_bytes(most(g1, nrep), recv.at[13])
        gsum = summed(g1, nrep)
        for q in range(ny):
            g2s[q, 0:yrows, :] = gsum[q * yrows:(q + 1) * yrows]
            g2s[q, yrows:yrows + 8, :] = gsum[wrows:]
        for t in others(y_axis):
            send_to(y_axis, t, g2s.at[t], g2.at[y], 14)
        g2[y] = g2s[y]
        wait_bytes(most(g2, ny), recv.at[14])
        g3s[...] = summed(g2, ny)
        for t in others(z_axis):
            send_to(z_axis, t, g3s, g3.at[z], 15)
        g3[z] = g3s[...]

        for h, axis in ((0, z_axis), (1, y_axis)):
            wait_bytes(most(b1.at[h], ny), recv.at[8 + h])
            acc = b1[h, 0].astype(F32)
            for q in range(1, ny):
                acc = acc + b1[h, q].astype(F32)
            acc = acc.reshape(hpos // ny * cs, width).astype(BF)
            back_swap = node_swap if cs == nz * half else swap_matrix(cs, nz * half)
            b2s[h] = dot(back_swap, acc).astype(BF).reshape(nz, half, cs, width)
            for t in others(axis):
                send_to(axis, t, b2s.at[h, t], b2.at[h, axis[1]], 10 + h)
            b2[h, axis[1]] = b2s[h, axis[1]]

        wait_bytes(most(g3, nz), recv.at[15])
        gfull = summed(g3, nz) * scale
        gb_o[...] = jnp.concatenate([gfull[yrows:yrows + 1], gfull[yrows + 1:yrows + 2]], axis=1)
        g4[y] = gfull[:yrows]
        for t in others(y_axis):
            send_to(y_axis, t, g4.at[y], g4.at[y], 16)

        for h in range(2):
            wait_bytes(most(b2.at[h], nz), recv.at[10 + h])
            acc = b2[h, 0].astype(F32)
            for q in range(1, nz):
                acc = acc + b2[h, q].astype(F32)
            r0[pl.ds(h * half, half)] = acc
        for b in range(nbd):
            node = b * blk + p * cs
            to = node // share
            slot = (node - to * share) // cs

            @pl.when(to == p)
            def _():
                pltpu.make_async_copy(r0.at[b], r1.at[slot], recv.at[12]).start()

            @pl.when(to != p)
            def _():
                send_to(rep_axis, to, r0.at[b], r1.at[slot], 12, 18 + b)

        wait_bytes(most(g4, ny), recv.at[16])
        g5[p] = g4[...].reshape(wrows, width)
        for t in others(rep_axis):
            send_to(rep_axis, t, g5.at[p], g5.at[p], 17)

        contract = lax.dot_general(dpre_b, w_self[...], contract_cols, preferred_element_type=F32)
        wait_bytes(r1, recv.at[12])
        gf_o[...] = contract + r1[...].reshape(share, width)
        wait_bytes(most(g5, nrep), recv.at[17])
        every = g5[...].reshape(4, width, width)
        for s in range(2):
            gs_o[:, s * width:(s + 1) * width] = every[s]
            gn_o[:, s * width:(s + 1) * width] = every[2 + s]

        wait_bytes(most(meta, nrep), send.at[0])
        wait_bytes(most(tt, nrep), send.at[1])
        for h in range(2):
            wait_bytes(most(f1.at[h], nz), send.at[2 + h])
            wait_bytes(most(f2.at[h], nz), send.at[4 + h])
            wait_bytes(most(b1.at[h], nz), send.at[8 + h])
            wait_bytes(most(b2.at[h], nz), send.at[10 + h])
        wait_bytes(most(a1, nrep), send.at[6])
        wait_bytes(most(dg, nrep), send.at[7])
        for b in range(nbd):
            node = b * blk + p * cs

            @pl.when(node // share != p)
            def _():
                wait_bytes(r0.at[b], send.at[18 + b])
        wait_bytes(most(g1, nrep), send.at[13])
        wait_bytes(most(g2, ny), send.at[14])
        wait_bytes(most(g3, nz), send.at[15])
        wait_bytes(most(g4, ny), send.at[16])
        wait_bytes(most(g5, nrep), send.at[17])

    V = pltpu.VMEM
    scratch = [
        V((8, tiles_all), jnp.int32),
        V((nrep, 8, tiles_all), jnp.int32),
        V((tpd, blk, blk), BF),
        V((nrep, cs, tpd, blk), BF),
        V((nrep, cs, tpd, blk), BF),
        V((2, nz, half, cs, width), BF),
        V((2, ny, cs, nz * half, width), BF),
        V((nodes, cs * tiles_all), BF),
        V((cs * tiles_all, width), BF),
        V((nrep, share, width), BF),
        V((nrep, share, width), BF),
        V((cs, npos, nodes), BF),
        V((share, width), BF),
        V((nrep, share, width), BF),
        V((2, ny, cs, nz * half, width), BF),
        V((2, ny, cs, nz * half, width), BF),
        V((2, nz, half, cs, width), BF),
        V((2, nz, half, cs, width), BF),
        V((nbd, cs, width), F32),
        V((share // cs, cs, width), F32),
        V((nrep, wrows + 8, width), F32),
        V((nrep, wrows + 8, width), F32),
        V((ny, yrows + 8, width), F32),
        V((ny, yrows + 8, width), F32),
        V((yrows + 8, width), F32),
        V((nz, yrows + 8, width), F32),
        V((ny, yrows, width), F32),
        V((nrep, wrows, width), F32),
        pltpu.SemaphoreType.DMA((22,)),
        pltpu.SemaphoreType.DMA((18,)),
    ]
    outs = (
        jax.ShapeDtypeStruct((share, hid), BF),
        jax.ShapeDtypeStruct((share, width), F32),
        jax.ShapeDtypeStruct((width, hid), F32),
        jax.ShapeDtypeStruct((width, hid), F32),
        jax.ShapeDtypeStruct((1, hid), F32),
    )
    vmem, smem = pl.BlockSpec(memory_space=pltpu.VMEM), pl.BlockSpec(memory_space=pltpu.SMEM)
    return pl.pallas_call(
        kernel,
        out_shape=outs,
        in_specs=[vmem, vmem, smem, smem, smem, vmem, vmem, vmem, vmem],
        out_specs=tuple([vmem] * 5),
        scratch_shapes=scratch,
        compiler_params=pltpu.CompilerParams(
            collective_id=0, has_side_effects=True, vmem_limit_bytes=56 * 1024 * 1024),
    )


def solution(mesh):
    nrow, nrep = mesh.shape["row"], mesh.shape["rep"]
    side = int(round(nrow ** 0.5))

    def per_device(features, edge_tiles, tile_owner, tile_block, tile_row, w_self, w_neigh,
                   bias_vector, cotangent):
        tpd, blk, _ = edge_tiles.shape
        nodes, width = features.shape
        hid = w_self.shape[1]
        nbd = nodes // blk
        call = make_kernel(side, nrow // side, nrep, tpd, blk, width, hid, nbd)
        hidden, gf, gs, gn, gb = call(
            features.reshape(nbd, blk, width), edge_tiles, tile_owner, tile_block, tile_row,
            w_self, w_neigh, bias_vector.reshape(1, hid), cotangent)
        return hidden, gf, gs, gn, gb.reshape(hid)

    in_specs = (
        P("row", None), P(("row", "rep"), None, None), P(("row", "rep"), None),
        P(("row", "rep")), P(("row", "rep")), P(), P(), P(), P(("row", "rep"), None),
    )
    out_specs = (P(("row", "rep"), None), P(("row", "rep"), None), P(), P(), P())
    return jax.shard_map(
        per_device, mesh=mesh, in_specs=in_specs, out_specs=out_specs, check_vma=False)
```

```python
import jax
import jax.numpy as jnp
from jax import lax
from jax.experimental import pallas as pl
from jax.experimental.pallas import tpu as pltpu
from jax.sharding import PartitionSpec as P

MESH = pl.DeviceIdType.MESH
BF = jnp.bfloat16
F32 = jnp.float32


def swap_matrix(first, second):
    size = first * second
    out = lax.broadcasted_iota(jnp.int32, (size, size), 0)
    src = lax.broadcasted_iota(jnp.int32, (size, size), 1)
    match = (out // first == src % second) & (out % first == src // second)
    return match.astype(F32).astype(BF)


def dot(a, b):
    return jnp.dot(a, b, preferred_element_type=F32)


def make_kernel(nz, ny, nrep, tpd, blk, width, hid, nbd):
    cs = blk // nrep
    nodes = nbd * blk
    share = nodes // nrep
    half = nbd // 2
    npos = nbd * nz * ny
    hpos = npos // 2
    tiles_all = nrep * tpd
    scale = float(nz * ny * nodes) ** -0.5
    assert nz == ny and hid == 2 * width
    wrows = 4 * width // nrep
    yrows = wrows // ny
    early = min(3, ny - 1)
    nx = nrep // 2

    def kernel(
        feat, tiles, owner, tblock, trow, w_self, w_neigh, bias, cot,
        hid_o, gf_o, gs_o, gn_o, gb_o,
        meta_s, meta, xt, ysend, tt, f1, f2, ttm, fg, a0, a1, dense, dg0, dg, o0, b1, b2s, b2,
        gl, g1, g2s, g2, g3s, g3, g4, g5, send, recv,
    ):
        row = lax.axis_index("row")
        p = lax.axis_index("rep")
        z = row // ny
        y = row - z * ny

        def on_rep(q):
            return (row, q)

        def on_z(q):
            return (q * ny + y, p)

        def on_y(q):
            return (z * ny + q, p)

        axes = ((nrep, p, on_rep), (nz, z, on_z), (ny, y, on_y))
        rep_axis, z_axis, y_axis = axes

        def far_first(n):
            order = []
            for d in range(n // 2, 0, -1):
                order += [d] if n - d == d else [d, n - d]
            return order

        def others(axis):
            n, me, _ = axis
            if axis is rep_axis:
                x = me // 2
                core = me - 2 * x
                return [lax.rem(x + d, nx) * 2 + lax.rem(core + e, 2)
                        for d in far_first(nx) + [0] for e in (0, 1) if d or e]
            return [lax.rem(me + d, n) for d in far_first(n)]

        def send_to(axis, t, src, dst, sem, left=None):
            pltpu.make_async_remote_copy(
                src_ref=src, dst_ref=dst, recv_sem=recv.at[sem],
                send_sem=send.at[sem if left is None else left],
                device_id=axis[2](t), device_id_type=MESH,
            ).start()

        def wait_bytes(ref, sem):
            pltpu.make_async_copy(ref, ref, sem).wait()

        def most(buf, n):
            return buf.at[pl.ds(0, n - 1)]

        barrier = pltpu.get_barrier_semaphore()
        count = 0
        for axis in axes:
            for t in others(axis):
                pl.semaphore_signal(barrier, inc=1, device_id=axis[2](t), device_id_type=MESH)
                count += 1

        lane = lax.broadcasted_iota(jnp.int32, (8, tiles_all), 1)
        code = jnp.zeros((8, tiles_all), jnp.int32)
        for k in range(tpd):
            own = owner[k]
            own_z = own // ny
            own_y = own - own_z * ny
            b = tblock[k]
            low = b - (b // half) * half
            first = own_y * (2 * nz) + own_z * half + low
            second = hpos + own_z * (2 * ny) + own_y * half + low
            where_to = jnp.where(b < half, first, second) + trow[k] * npos
            code = jnp.where(lane == p * tpd + k, where_to, code)
        meta_s[...] = code

        pl.semaphore_wait(barrier, count)

        start = pl.multiple_of(p * cs, cs)
        f1[0, z] = feat[pl.ds(0, half), pl.ds(start, cs), :]
        f1[1, y] = feat[pl.ds(half, half), pl.ds(start, cs), :]
        for h, axis in ((0, z_axis), (1, y_axis)):
            for t in others(axis):
                send_to(axis, t, feat.at[pl.ds(h * half, half), pl.ds(start, cs), :],
                        f1.at[h, axis[1]], 2 + h)
        for t in others(rep_axis):
            send_to(rep_axis, t, meta_s, meta.at[p], 0)
        meta[p] = code

        for k in range(tpd):
            xt[k] = tiles[k].T
        tile_swap = swap_matrix(tpd, cs)
        node_swap = swap_matrix(nz * half, cs)

        def columns_of(t):
            part = xt[:, pl.ds(pl.multiple_of(t * cs, cs), cs), :].reshape(tpd * cs, blk)
            return dot(tile_swap, part).astype(BF).reshape(cs, tpd, blk)

        for t in others(rep_axis):
            ysend[t] = columns_of(t)
            send_to(rep_axis, t, ysend.at[t], tt.at[p], 1)
        tt[p] = columns_of(p)

        for h, axis in ((0, y_axis), (1, z_axis)):
            wait_bytes(most(f1.at[h], nz), recv.at[2 + h])
            part = dot(node_swap, f1[h].reshape(hpos // ny * cs, width)).astype(BF)
            f2[h, axis[1]] = part.reshape(cs, nz * half, width)
            for t in others(axis):
                send_to(axis, t, f2.at[h, axis[1]], f2.at[h, axis[1]], 4 + h)

        wait_bytes(most(meta, nrep), recv.at[0])
        codes = meta[0]
        for q in range(1, nrep):
            codes = codes + meta[q]
        codes = codes[0:1, :]
        rows_of = codes // npos
        pos = codes - rows_of * npos
        wait_bytes(most(tt, nrep), recv.at[1])
        for c in range(cs):
            turned = tt[:, c].reshape(tiles_all, blk).T
            for n in range(nbd):
                ttm[n * blk:(n + 1) * blk, c * tiles_all:(c + 1) * tiles_all] = jnp.where(
                    rows_of == n, turned, jnp.zeros_like(turned))
        pos_iota = lax.broadcasted_iota(jnp.int32, (npos, tiles_all), 0)
        select = (pos_iota == pos).astype(F32).T.astype(BF)

        for h in range(2):
            wait_bytes(most(f2.at[h], ny), recv.at[4 + h])
        for c in range(cs):
            here = jnp.concatenate(
                [f2[0, :, c].reshape(hpos, width), f2[1, :, c].reshape(hpos, width)], axis=0)
            fg[c * tiles_all:(c + 1) * tiles_all, :] = dot(select, here).astype(BF)
        partial = dot(ttm[...], fg[...]).astype(BF).reshape(nrep, share, width)
        a0[...] = partial
        for t in others(rep_axis):
            send_to(rep_axis, t, a0.at[t], a1.at[p], 6)
        a1[p] = a0[p]

        spread = jnp.concatenate(
            [(pos_iota + n * npos == codes).astype(F32).astype(BF) for n in range(nbd)], axis=0)
        for c in range(cs):
            placed = dot(spread, tt[:, c].reshape(tiles_all, blk)).astype(BF)
            for n in range(nbd):
                for h in range(2):
                    at = n * npos + h * hpos
                    dense[h, :, c, :, n * blk:(n + 1) * blk] = placed[at:at + hpos].reshape(
                        ny, nz * half, blk)

        per_block = blk // share if share < blk else 1
        if share < blk:
            which = p // per_block
            inside = pl.multiple_of((p - which * per_block) * share, share)
            own = feat[which, pl.ds(inside, share), :]
        else:
            own = feat[pl.ds(p * (share // blk), share // blk)].reshape(share, width)
        own_part = dot(own, w_self[...]) + bias[...]

        wait_bytes(most(a1, nrep), recv.at[6])
        total = a1[0].astype(F32)
        for q in range(1, nrep):
            total = total + a1[q].astype(F32)
        agg = total.astype(BF)
        pre = own_part + dot(agg, w_neigh[...])
        sig = jax.nn.sigmoid(pre)
        dpre = cot[...].astype(F32) * sig * (1.0 + pre * (1.0 - sig))
        dpre_b = dpre.astype(BF)
        contract_cols = (((1,), (1,)), ((), ()))
        dagg = lax.dot_general(dpre_b, w_neigh[...], contract_cols, preferred_element_type=F32)
        dg0[...] = dagg.astype(BF)
        for t in others(rep_axis):
            send_to(rep_axis, t, dg0, dg.at[p], 7)
        dg[p] = dg0[...]
        hid_o[...] = (pre * sig).astype(BF)

        contract_rows = (((0,), (0,)), ((), ()))
        bsum = jnp.sum(dpre, axis=0, keepdims=True)
        high = bsum.astype(BF).astype(F32)
        row16 = lax.broadcasted_iota(jnp.int32, (16, width), 0)
        bias_rows = jnp.zeros((16, width), F32)
        for at, part in ((0, high), (8, bsum - high)):
            for s in range(2):
                bias_rows = jnp.where(row16 == at + s, part[:, s * width:(s + 1) * width], bias_rows)
        bias_rows = bias_rows.astype(BF)
        both = jnp.concatenate([own, agg], axis=1)
        grads = lax.dot_general(both, dpre_b, contract_rows, preferred_element_type=F32)
        pieces = jnp.concatenate(
            [grads[w * width:(w + 1) * width, s * width:(s + 1) * width]
             for w in range(2) for s in range(2)], axis=0)
        for q in range(nrep):
            gl[q, 0:wrows, :] = pieces[q * wrows:(q + 1) * wrows].astype(BF)
            gl[q, wrows:wrows + 16, :] = bias_rows
        for t in others(rep_axis):
            send_to(rep_axis, t, gl.at[t], g1.at[p], 13)
        g1[p] = gl[p]

        def summed(buf, n):
            acc = buf[0].astype(F32)
            for q in range(1, n):
                acc = acc + buf[q].astype(F32)
            return acc

        wait_bytes(most(dg, nrep), recv.at[7])
        dall = dg[...].reshape(nodes, width)
        by_half = ((0, y_axis), (1, z_axis))

        def back_piece(h, t):
            flat = dense[h, t].reshape(cs * nz * half, nodes)
            return dot(flat, dall).astype(BF).reshape(cs, nz * half, width)

        def back_send(first, last):
            for i in range(first, last):
                for h, axis in by_half:
                    t = others(axis)[i]
                    o0[h, t] = back_piece(h, t)
                    send_to(axis, t, o0.at[h, t], b1.at[h, axis[1]], 8 + h)

        back_send(0, 1)

        wait_bytes(most(g1, nrep), recv.at[13])
        gsum = summed(g1, nrep)
        gbias = gsum[wrows:wrows + 8] + gsum[wrows + 8:wrows + 16]
        for q in range(ny):
            g2s[q, 0:yrows, :] = gsum[q * yrows:(q + 1) * yrows]
            g2s[q, yrows:yrows + 8, :] = gbias
        for t in others(y_axis):
            send_to(y_axis, t, g2s.at[t], g2.at[y], 14)
        g2[y] = g2s[y]
        back_send(1, early)

        wait_bytes(most(g2, ny), recv.at[14])
        g3s[...] = summed(g2, ny)
        for t in others(z_axis):
            send_to(z_axis, t, g3s, g3.at[z], 15)
        g3[z] = g3s[...]
        back_send(early, ny - 1)
        for h, axis in by_half:
            b1[h, axis[1]] = back_piece(h, axis[1])

        contract = lax.dot_general(dpre_b, w_self[...], contract_cols, preferred_element_type=F32)
        wait_bytes(most(g3, nz), recv.at[15])
        gfull = summed(g3, nz) * scale
        gb_o[...] = jnp.concatenate([gfull[yrows:yrows + 1], gfull[yrows + 1:yrows + 2]], axis=1)
        g4[y] = gfull[:yrows]
        for t in others(y_axis):
            send_to(y_axis, t, g4.at[y], g4.at[y], 16)

        back_swap = node_swap if cs == nz * half else swap_matrix(cs, nz * half)
        for h, axis in ((0, z_axis), (1, y_axis)):
            wait_bytes(most(b1.at[h], ny), recv.at[8 + h])
            acc = summed(b1.at[h], ny).reshape(hpos // ny * cs, width).astype(BF)
            b2s[h] = dot(back_swap, acc).astype(BF).reshape(nz, half, cs, width)
            for t in others(axis) + [None]:
                for low in range(half):
                    b = h * half + low
                    node = b * blk + p * cs
                    to = node // share
                    slot = (node - to * share) // cs
                    into = b2.at[axis[1], slot]
                    if t is not None:
                        place = (t * ny + y, to) if h == 0 else (z * ny + t, to)
                        pltpu.make_async_remote_copy(
                            src_ref=b2s.at[h, t, low], dst_ref=into, send_sem=send.at[10],
                            recv_sem=recv.at[10], device_id=place, device_id_type=MESH,
                        ).start()
                        continue

                    mine = b2s.at[h, axis[1], low]

                    @pl.when(to == p)
                    def _():
                        pltpu.make_async_copy(mine, into, recv.at[10]).start()

                    @pl.when(to != p)
                    def _():
                        send_to(rep_axis, to, mine, into, 10, 18 + b)

        wait_bytes(most(g4, ny), recv.at[16])
        g5[p] = g4[...].reshape(wrows, width).astype(BF)
        for t in others(rep_axis):
            send_to(rep_axis, t, g5.at[p], g5.at[p], 17)

        wait_bytes(b2, recv.at[10])
        gf_o[...] = contract + summed(b2, nz).reshape(share, width)
        wait_bytes(most(g5, nrep), recv.at[17])
        every = g5[...].reshape(4, width, width).astype(F32)
        for s in range(2):
            gs_o[:, s * width:(s + 1) * width] = every[s]
            gn_o[:, s * width:(s + 1) * width] = every[2 + s]

        wait_bytes(most(meta, nrep), send.at[0])
        wait_bytes(most(tt, nrep), send.at[1])
        for h in range(2):
            wait_bytes(most(f1.at[h], nz), send.at[2 + h])
            wait_bytes(most(f2.at[h], nz), send.at[4 + h])
            wait_bytes(most(b1.at[h], nz), send.at[8 + h])
        wait_bytes(most(a1, nrep), send.at[6])
        wait_bytes(most(dg, nrep), send.at[7])
        wait_bytes(most(b2, nz), send.at[10])
        for b in range(nbd):
            node = b * blk + p * cs

            @pl.when(node // share != p)
            def _():
                wait_bytes(b2s.at[0, 0, 0], send.at[18 + b])
        wait_bytes(most(g1, nrep), send.at[13])
        wait_bytes(most(g2, ny), send.at[14])
        wait_bytes(most(g3, nz), send.at[15])
        wait_bytes(most(g4, ny), send.at[16])
        wait_bytes(most(g5, nrep), send.at[17])

    V = pltpu.VMEM
    scratch = [
        V((8, tiles_all), jnp.int32),
        V((nrep, 8, tiles_all), jnp.int32),
        V((tpd, blk, blk), BF),
        V((nrep, cs, tpd, blk), BF),
        V((nrep, cs, tpd, blk), BF),
        V((2, nz, half, cs, width), BF),
        V((2, ny, cs, nz * half, width), BF),
        V((nodes, cs * tiles_all), BF),
        V((cs * tiles_all, width), BF),
        V((nrep, share, width), BF),
        V((nrep, share, width), BF),
        V((2, ny, cs, nz * half, nodes), BF),
        V((share, width), BF),
        V((nrep, share, width), BF),
        V((2, ny, cs, nz * half, width), BF),
        V((2, ny, cs, nz * half, width), BF),
        V((2, nz, half, cs, width), BF),
        V((nz, share // cs, cs, width), BF),
        V((nrep, wrows + 16, width), BF),
        V((nrep, wrows + 16, width), BF),
        V((ny, yrows + 8, width), F32),
        V((ny, yrows + 8, width), F32),
        V((yrows + 8, width), F32),
        V((nz, yrows + 8, width), F32),
        V((ny, yrows, width), F32),
        V((nrep, wrows, width), BF),
        pltpu.SemaphoreType.DMA((22,)),
        pltpu.SemaphoreType.DMA((18,)),
    ]
    outs = (
        jax.ShapeDtypeStruct((share, hid), BF),
        jax.ShapeDtypeStruct((share, width), F32),
        jax.ShapeDtypeStruct((width, hid), F32),
        jax.ShapeDtypeStruct((width, hid), F32),
        jax.ShapeDtypeStruct((1, hid), F32),
    )
    vmem, smem = pl.BlockSpec(memory_space=pltpu.VMEM), pl.BlockSpec(memory_space=pltpu.SMEM)
    return pl.pallas_call(
        kernel,
        out_shape=outs,
        in_specs=[vmem, vmem, smem, smem, smem, vmem, vmem, vmem, vmem],
        out_specs=tuple([vmem] * 5),
        scratch_shapes=scratch,
        compiler_params=pltpu.CompilerParams(
            collective_id=0, has_side_effects=True, vmem_limit_bytes=56 * 1024 * 1024),
    )


def finish(results):
    def kernel(*refs):
        n = len(results)
        copies = [pltpu.make_async_copy(refs[i], refs[n + i], refs[2 * n].at[i]) for i in range(n)]
        for copy in copies:
            copy.start()
        for copy in copies:
            copy.wait()

    anywhere = pl.BlockSpec(memory_space=pl.ANY)
    return pl.pallas_call(
        kernel,
        out_shape=tuple(jax.ShapeDtypeStruct(r.shape, r.dtype) for r in results),
        in_specs=[pl.BlockSpec(memory_space=pltpu.VMEM)] * len(results),
        out_specs=tuple([anywhere] * len(results)),
        scratch_shapes=[pltpu.SemaphoreType.DMA((len(results),))],
    )(*results)


def solution(mesh):
    nrow, nrep = mesh.shape["row"], mesh.shape["rep"]
    side = int(round(nrow ** 0.5))

    def per_device(features, edge_tiles, tile_owner, tile_block, tile_row, w_self, w_neigh,
                   bias_vector, cotangent):
        tpd, blk, _ = edge_tiles.shape
        nodes, width = features.shape
        hid = w_self.shape[1]
        nbd = nodes // blk
        call = make_kernel(side, nrow // side, nrep, tpd, blk, width, hid, nbd)
        results = call(
            features.reshape(nbd, blk, width), edge_tiles, tile_owner.reshape(tpd), tile_block, tile_row,
            w_self, w_neigh, bias_vector.reshape(1, hid), cotangent)
        hidden, gf, gs, gn, gb = finish(results)
        return hidden, gf, gs, gn, gb.reshape(hid)

    in_specs = (
        P("row", None), P(("row", "rep"), None, None), P(("row", "rep"), None),
        P(("row", "rep")), P(("row", "rep")), P(), P(), P(), P(("row", "rep"), None),
    )
    out_specs = (P(("row", "rep"), None), P(("row", "rep"), None), P(), P(), P())
    return jax.shard_map(
        per_device, mesh=mesh, in_specs=in_specs, out_specs=out_specs, check_vma=False)
```

```python
import jax
import jax.numpy as jnp
from jax import lax
from jax.experimental import pallas as pl
from jax.experimental.pallas import tpu as pltpu
from jax.sharding import PartitionSpec as P

MESH = pl.DeviceIdType.MESH
BF = jnp.bfloat16
F32 = jnp.float32


def swap_matrix(first, second):
    size = first * second
    out = lax.broadcasted_iota(jnp.int32, (size, size), 0)
    src = lax.broadcasted_iota(jnp.int32, (size, size), 1)
    match = (out // first == src % second) & (out % first == src // second)
    return match.astype(F32).astype(BF)


def dot(a, b):
    return jnp.dot(a, b, preferred_element_type=F32)


def make_kernel(nz, ny, nrep, tpd, blk, width, hid, nbd):
    cs = blk // nrep
    nodes = nbd * blk
    share = nodes // nrep
    half = nbd // 2
    npos = nbd * nz * ny
    hpos = npos // 2
    tiles_all = nrep * tpd
    scale = float(nz * ny * nodes) ** -0.5
    assert nz == ny == 8 and hid == 2 * width
    grows = 2 * width // ny
    F2, P2, M2, B1, RL, RP, RM, GA, GB, GD = range(20, 40, 2)
    GC = 13
    nx = nrep // 2

    def kernel(
        feat, tiles, owner, tblock, trow, w_self, w_neigh, bias, cot,
        hid_o, gf_o, gs_o, gn_o, gb_o,
        meta_s, meta, xt, ysend, tt, f1, f2, ttm, fg, a0, a1, dense, dg0, dg, o0, b1, b2s, b2,
        ga0, ga, gb0, gb, gc0, gc, gd, relay, kept, send, recv,
    ):
        row = lax.axis_index("row")
        p = lax.axis_index("rep")
        z = row // ny
        y = row - z * ny

        def on_rep(q):
            return (row, q)

        def on_z(q):
            return (q * ny + y, p)

        def on_y(q):
            return (z * ny + q, p)

        axes = ((nrep, p, on_rep), (nz, z, on_z), (ny, y, on_y))
        rep_axis, z_axis, y_axis = axes

        def far_first(n):
            order = []
            for d in range(n // 2, 0, -1):
                order += [d] if n - d == d else [d, n - d]
            return order

        def others(axis):
            n, me, _ = axis
            if axis is rep_axis:
                x = me // 2
                core = me - 2 * x
                return [lax.rem(x + d, nx) * 2 + lax.rem(core + e, 2)
                        for d in far_first(nx) + [0] for e in (0, 1) if d or e]
            return [lax.rem(me + d, n) for d in far_first(n)]

        def off(axis, d):
            return lax.rem(axis[1] + (d + axis[0]), axis[0])

        def send_to(axis, t, src, dst, sem, left=None):
            pltpu.make_async_remote_copy(
                src_ref=src, dst_ref=dst, recv_sem=recv.at[sem],
                send_sem=send.at[sem if left is None else left],
                device_id=axis[2](t), device_id_type=MESH,
            ).start()

        def wait_bytes(ref, sem):
            pltpu.make_async_copy(ref, ref, sem).wait()

        def most(buf, n):
            return buf.at[pl.ds(0, n - 1)]

        barrier = pltpu.get_barrier_semaphore()
        count = 0
        for axis in axes:
            for t in others(axis):
                pl.semaphore_signal(barrier, inc=1, device_id=axis[2](t), device_id_type=MESH)
                count += 1

        lane = lax.broadcasted_iota(jnp.int32, (8, tiles_all), 1)
        code = jnp.zeros((8, tiles_all), jnp.int32)
        for k in range(tpd):
            own = owner[k]
            own_z = own // ny
            own_y = own - own_z * ny
            b = tblock[k]
            low = b - (b // half) * half
            first = own_y * (2 * nz) + own_z * half + low
            second = hpos + own_z * (2 * ny) + own_y * half + low
            where_to = jnp.where(b < half, first, second) + trow[k] * npos
            code = jnp.where(lane == p * tpd + k, where_to, code)
        meta_s[...] = code

        pl.semaphore_wait(barrier, count)

        start = pl.multiple_of(p * cs, cs)
        f1[0, z] = feat[pl.ds(0, half), pl.ds(start, cs), :]
        f1[1, y] = feat[pl.ds(half, half), pl.ds(start, cs), :]
        for h, axis in ((0, z_axis), (1, y_axis)):
            for t in others(axis):
                send_to(axis, t, feat.at[pl.ds(h * half, half), pl.ds(start, cs), :],
                        f1.at[h, axis[1]], 2 + h)
        for t in others(rep_axis):
            send_to(rep_axis, t, meta_s, meta.at[p], 0)
        meta[p] = code

        for k in range(tpd):
            xt[k] = tiles[k].T
        tile_swap = swap_matrix(tpd, cs)
        node_swap = swap_matrix(nz * half, cs)

        def columns_of(t):
            part = xt[:, pl.ds(pl.multiple_of(t * cs, cs), cs), :].reshape(tpd * cs, blk)
            return dot(tile_swap, part).astype(BF).reshape(cs, tpd, blk)

        for t in others(rep_axis):
            ysend[t] = columns_of(t)
            send_to(rep_axis, t, ysend.at[t], tt.at[p], 1)
        tt[p] = columns_of(p)

        for h, axis in ((0, y_axis), (1, z_axis)):
            wait_bytes(most(f1.at[h], nz), recv.at[2 + h])
            part = dot(node_swap, f1[h].reshape(hpos // ny * cs, width)).astype(BF)
            me = axis[1]
            f2[h, me] = part.reshape(cs, nz * half, width)
            for d in (2, -2, 1, -1):
                sem = {2: M2, -2: P2}.get(d, F2) + h
                send_to(axis, off(axis, d), f2.at[h, me], f2.at[h, me], sem, F2 + h)
        for sem, d in ((P2, 2), (M2, -2)):
            for h, axis in ((0, y_axis), (1, z_axis)):
                there = off(axis, d)
                wait_bytes(f2.at[h, there], recv.at[sem + h])
                whole = f2.at[h, there]
                send_to(axis, off(axis, -d // 2), whole, whole, F2 + h)
                part = f2.at[h, there, pl.ds(0 if d > 0 else cs // 2, cs // 2)]
                send_to(axis, off(axis, -d), part, part, F2 + h)

        wait_bytes(most(meta, nrep), recv.at[0])
        codes = meta[0]
        for q in range(1, nrep):
            codes = codes + meta[q]
        codes = codes[0:1, :]
        rows_of = codes // npos
        pos = codes - rows_of * npos
        wait_bytes(most(tt, nrep), recv.at[1])
        for c in range(cs):
            turned = tt[:, c].reshape(tiles_all, blk).T
            for n in range(nbd):
                ttm[n * blk:(n + 1) * blk, c * tiles_all:(c + 1) * tiles_all] = jnp.where(
                    rows_of == n, turned, jnp.zeros_like(turned))
        pos_iota = lax.broadcasted_iota(jnp.int32, (npos, tiles_all), 0)
        select = (pos_iota == pos).astype(F32).T.astype(BF)

        for h in range(2):
            wait_bytes(f2.at[h, pl.ds(0, 5)], recv.at[F2 + h])
        for c in range(cs):
            here = jnp.concatenate(
                [f2[0, :, c].reshape(hpos, width), f2[1, :, c].reshape(hpos, width)], axis=0)
            fg[c * tiles_all:(c + 1) * tiles_all, :] = dot(select, here).astype(BF)
        partial = dot(ttm[...], fg[...]).astype(BF).reshape(nrep, share, width)
        a0[...] = partial
        for t in others(rep_axis):
            send_to(rep_axis, t, a0.at[t], a1.at[p], 6)
        a1[p] = a0[p]

        spread = jnp.concatenate(
            [(pos_iota + n * npos == codes).astype(F32).astype(BF) for n in range(nbd)], axis=0)
        for c in range(cs):
            placed = dot(spread, tt[:, c].reshape(tiles_all, blk)).astype(BF)
            for n in range(nbd):
                for h in range(2):
                    at = n * npos + h * hpos
                    dense[h, :, c, :, n * blk:(n + 1) * blk] = placed[at:at + hpos].reshape(
                        ny, nz * half, blk)

        per_block = blk // share if share < blk else 1
        if share < blk:
            which = p // per_block
            inside = pl.multiple_of((p - which * per_block) * share, share)
            own = feat[which, pl.ds(inside, share), :]
        else:
            own = feat[pl.ds(p * (share // blk), share // blk)].reshape(share, width)
        own_part = dot(own, w_self[...]) + bias[...]

        wait_bytes(most(a1, nrep), recv.at[6])
        total = a1[0].astype(F32)
        for q in range(1, nrep):
            total = total + a1[q].astype(F32)
        agg = total.astype(BF)
        pre = own_part + dot(agg, w_neigh[...])
        sig = jax.nn.sigmoid(pre)
        dpre = cot[...].astype(F32) * sig * (1.0 + pre * (1.0 - sig))
        dpre_b = dpre.astype(BF)
        contract_cols = (((1,), (1,)), ((), ()))
        dagg = lax.dot_general(dpre_b, w_neigh[...], contract_cols, preferred_element_type=F32)
        dg0[...] = dagg.astype(BF)
        for t in others(rep_axis):
            send_to(rep_axis, t, dg0, dg.at[p], 7)
        dg[p] = dg0[...]
        hid_o[...] = (pre * sig).astype(BF)

        def summed(buf, n):
            acc = buf[0].astype(F32)
            for q in range(1, n):
                acc = acc + buf[q].astype(F32)
            return acc

        def two_parts(value):
            high = value.astype(BF).astype(F32)
            return jnp.concatenate([high, value - high], axis=0).astype(BF)

        by_half = ((0, y_axis), (1, z_axis))
        by_other = ((0, z_axis), (1, y_axis))
        contract_rows = (((0,), (0,)), ((), ()))
        bsum = jnp.sum(dpre, axis=0, keepdims=True)
        row8 = lax.broadcasted_iota(jnp.int32, (8, width), 0)
        bias_rows = two_parts(jnp.where(
            row8 == 0, bsum[:, :width], jnp.where(row8 == 1, bsum[:, width:], 0.0)))
        for h, left in ((0, own), (1, agg)):
            grads = lax.dot_general(left, dpre_b, contract_rows, preferred_element_type=F32)
            grads = jnp.concatenate([grads[:, :width], grads[:, width:]], axis=0).astype(BF)
            for q in range(ny):
                ga0[h, q, 0:grows, :] = grads[q * grows:(q + 1) * grows]
                if h == 0:
                    ga0[h, q, grows:, :] = bias_rows
        rows_in = (grows + 16, grows)
        for h, axis in by_half:
            for t in others(axis):
                send_to(axis, t, ga0.at[h, t, pl.ds(0, rows_in[h])],
                        ga.at[h, axis[1], pl.ds(0, rows_in[h])], GA + h)
            ga[h, axis[1]] = ga0[h, axis[1]]

        contract = lax.dot_general(dpre_b, w_self[...], contract_cols, preferred_element_type=F32)

        wait_bytes(most(dg, nrep), recv.at[7])
        dall = dg[...].reshape(nodes, width)
        hc = cs // 2

        def back_piece(h, t):
            flat = dense[h, t].reshape(cs * nz * half, nodes)
            return dot(flat, dall).reshape(cs, nz * half, width)

        for h, axis in by_half:
            t = off(axis, 4)
            o0[h, t] = back_piece(h, t).astype(BF)
            send_to(axis, off(axis, 2), o0.at[h, t, pl.ds(0, hc)],
                    relay.at[h, 0, pl.ds(cs, hc)], RP + h, RL + h)
            send_to(axis, off(axis, -2), o0.at[h, t, pl.ds(hc, hc)],
                    relay.at[h, 1, pl.ds(cs, hc)], RM + h, RL + h)
        for h, axis in by_half:
            for d, sem in ((3, RP), (-3, RM)):
                t = off(axis, d)
                o0[h, t] = back_piece(h, t).astype(BF)
                send_to(axis, off(axis, d // 3), o0.at[h, t],
                        relay.at[h, 0 if d > 0 else 1, pl.ds(0, cs)], sem + h, RL + h)

        for h, axis in by_half:
            wait_bytes(ga.at[h, pl.ds(0, ny - 1), pl.ds(0, rows_in[h])], recv.at[GA + h])
            acc = summed(ga.at[h, :, pl.ds(0, rows_in[h])], ny)
            gb0[h, 0:grows] = acc[:grows].astype(BF)
            if h == 0:
                gb0[h, grows:] = two_parts(acc[grows:grows + 8] + acc[grows + 8:])
        for h, axis in by_other:
            for t in others(axis):
                send_to(axis, t, gb0.at[h, pl.ds(0, rows_in[h])],
                        gb.at[h, axis[1], pl.ds(0, rows_in[h])], GB + h)
            gb[h, axis[1]] = gb0[h]

        for h, axis in by_half:
            for d, slot in ((1, 0), (-1, 1)):
                t = off(axis, d)
                o0[h, t] = back_piece(h, t).astype(BF)
                send_to(axis, t, o0.at[h, t], b1.at[h, slot], B1 + h)
        for h, axis in by_half:
            for d, way, sem in ((2, 0, RP), (-2, 1, RM)):
                t = off(axis, d)
                made = back_piece(h, t)
                wait_bytes(relay.at[h, way], recv.at[sem + h])
                passed = relay[h, way].astype(F32)
                low, high = made[:hc] + passed[:hc], made[hc:] + passed[hc:cs]
                if d > 0:
                    low = low + passed[cs:]
                else:
                    high = high + passed[cs:]
                o0[h, t, 0:hc] = low.astype(BF)
                o0[h, t, hc:cs] = high.astype(BF)
                send_to(axis, t, o0.at[h, t], b1.at[h, 2 + way], B1 + h)
        for h, axis in by_half:
            kept[h] = back_piece(h, axis[1])

        for h, axis in by_other:
            wait_bytes(gb.at[h, pl.ds(0, nz - 1), pl.ds(0, rows_in[h])], recv.at[GB + h])
            acc = summed(gb.at[h, :, pl.ds(0, rows_in[h])], nz)
            gc0[h * grows:(h + 1) * grows] = acc[:grows].astype(BF)
            if h == 0:
                gc0[2 * grows:] = two_parts(acc[grows:grows + 8] + acc[grows + 8:])
        for t in others(rep_axis):
            send_to(rep_axis, t, gc0, gc.at[p], GC)
        gc[p] = gc0[...]

        back_swap = node_swap if cs == nz * half else swap_matrix(cs, nz * half)
        for h, axis in ((0, z_axis), (1, y_axis)):
            wait_bytes(b1.at[h], recv.at[B1 + h])
            acc = (kept[h] + summed(b1.at[h], 4)).reshape(hpos // ny * cs, width).astype(BF)
            b2s[h] = dot(back_swap, acc).astype(BF).reshape(nz, half, cs, width)
            for t in others(axis) + [None]:
                for low in range(half):
                    b = h * half + low
                    node = b * blk + p * cs
                    to = node // share
                    slot = (node - to * share) // cs
                    into = b2.at[axis[1], slot]
                    if t is not None:
                        place = (t * ny + y, to) if h == 0 else (z * ny + t, to)
                        pltpu.make_async_remote_copy(
                            src_ref=b2s.at[h, t, low], dst_ref=into, send_sem=send.at[10],
                            recv_sem=recv.at[10], device_id=place, device_id_type=MESH,
                        ).start()
                        continue

                    mine = b2s.at[h, axis[1], low]

                    @pl.when(to == p)
                    def _():
                        pltpu.make_async_copy(mine, into, recv.at[10]).start()

                    @pl.when(to != p)
                    def _():
                        send_to(rep_axis, to, mine, into, 10, 18 + b)

        wait_bytes(most(gc, nrep), recv.at[GC])
        acc = summed(gc, nrep) * scale
        gbias = acc[2 * grows:2 * grows + 8] + acc[2 * grows + 8:]
        gb_o[...] = jnp.concatenate([gbias[0:1], gbias[1:2]], axis=1)
        for h, axis in by_half:
            me = axis[1]
            gd[h, me] = acc[h * grows:(h + 1) * grows].astype(BF)
            for t in others(axis):
                send_to(axis, t, gd.at[h, me], gd.at[h, me], GD + h)

        wait_bytes(b2, recv.at[10])
        gf_o[...] = contract + summed(b2, nz).reshape(share, width)
        for h, out in ((0, gs_o), (1, gn_o)):
            wait_bytes(most(gd.at[h], ny), recv.at[GD + h])
            every = gd[h].reshape(2, width, width).astype(F32)
            for c in range(2):
                out[:, c * width:(c + 1) * width] = every[c]

        wait_bytes(most(meta, nrep), send.at[0])
        wait_bytes(most(tt, nrep), send.at[1])
        for h in range(2):
            wait_bytes(most(f1.at[h], nz), send.at[2 + h])
            wait_bytes(most(f2.at[h], nz), send.at[F2 + h])
            wait_bytes(relay.at[h], send.at[RL + h])
            wait_bytes(b1.at[h], send.at[B1 + h])
            wait_bytes(ga.at[h, pl.ds(0, ny - 1), pl.ds(0, rows_in[h])], send.at[GA + h])
            wait_bytes(gb.at[h, pl.ds(0, nz - 1), pl.ds(0, rows_in[h])], send.at[GB + h])
            wait_bytes(most(gd.at[h], ny), send.at[GD + h])
        wait_bytes(most(a1, nrep), send.at[6])
        wait_bytes(most(dg, nrep), send.at[7])
        wait_bytes(most(b2, nz), send.at[10])
        for b in range(nbd):
            node = b * blk + p * cs

            @pl.when(node // share != p)
            def _():
                wait_bytes(b2s.at[0, 0, 0], send.at[18 + b])
        wait_bytes(most(gc, nrep), send.at[GC])

    V = pltpu.VMEM
    scratch = [
        V((8, tiles_all), jnp.int32),
        V((nrep, 8, tiles_all), jnp.int32),
        V((tpd, blk, blk), BF),
        V((nrep, cs, tpd, blk), BF),
        V((nrep, cs, tpd, blk), BF),
        V((2, nz, half, cs, width), BF),
        V((2, ny, cs, nz * half, width), BF),
        V((nodes, cs * tiles_all), BF),
        V((cs * tiles_all, width), BF),
        V((nrep, share, width), BF),
        V((nrep, share, width), BF),
        V((2, ny, cs, nz * half, nodes), BF),
        V((share, width), BF),
        V((nrep, share, width), BF),
        V((2, ny, cs, nz * half, width), BF),
        V((2, 4, cs, nz * half, width), BF),
        V((2, nz, half, cs, width), BF),
        V((nz, share // cs, cs, width), BF),
        V((2, ny, grows + 16, width), BF),
        V((2, ny, grows + 16, width), BF),
        V((2, grows + 16, width), BF),
        V((2, nz, grows + 16, width), BF),
        V((2 * grows + 16, width), BF),
        V((nrep, 2 * grows + 16, width), BF),
        V((2, ny, grows, width), BF),
        V((2, 2, cs + cs // 2, nz * half, width), BF),
        V((2, cs, nz * half, width), F32),
        pltpu.SemaphoreType.DMA((40,)),
        pltpu.SemaphoreType.DMA((40,)),
    ]
    outs = (
        jax.ShapeDtypeStruct((share, hid), BF),
        jax.ShapeDtypeStruct((share, width), F32),
        jax.ShapeDtypeStruct((width, hid), F32),
        jax.ShapeDtypeStruct((width, hid), F32),
        jax.ShapeDtypeStruct((1, hid), F32),
    )
    vmem, smem = pl.BlockSpec(memory_space=pltpu.VMEM), pl.BlockSpec(memory_space=pltpu.SMEM)
    return pl.pallas_call(
        kernel,
        out_shape=outs,
        in_specs=[vmem, vmem, smem, smem, smem, vmem, vmem, vmem, vmem],
        out_specs=tuple([vmem] * 5),
        scratch_shapes=scratch,
        compiler_params=pltpu.CompilerParams(
            collective_id=0, has_side_effects=True, vmem_limit_bytes=56 * 1024 * 1024),
    )


def finish(results):
    def kernel(*refs):
        n = len(results)
        copies = [pltpu.make_async_copy(refs[i], refs[n + i], refs[2 * n].at[i]) for i in range(n)]
        for copy in copies:
            copy.start()
        for copy in copies:
            copy.wait()

    anywhere = pl.BlockSpec(memory_space=pl.ANY)
    return pl.pallas_call(
        kernel,
        out_shape=tuple(jax.ShapeDtypeStruct(r.shape, r.dtype) for r in results),
        in_specs=[pl.BlockSpec(memory_space=pltpu.VMEM)] * len(results),
        out_specs=tuple([anywhere] * len(results)),
        scratch_shapes=[pltpu.SemaphoreType.DMA((len(results),))],
    )(*results)


def solution(mesh):
    nrow, nrep = mesh.shape["row"], mesh.shape["rep"]
    side = int(round(nrow ** 0.5))

    def per_device(features, edge_tiles, tile_owner, tile_block, tile_row, w_self, w_neigh,
                   bias_vector, cotangent):
        tpd, blk, _ = edge_tiles.shape
        nodes, width = features.shape
        hid = w_self.shape[1]
        nbd = nodes // blk
        call = make_kernel(side, nrow // side, nrep, tpd, blk, width, hid, nbd)
        results = call(
            features.reshape(nbd, blk, width), edge_tiles, tile_owner.reshape(tpd), tile_block, tile_row,
            w_self, w_neigh, bias_vector.reshape(1, hid), cotangent)
        hidden, gf, gs, gn, gb = finish(results)
        return hidden, gf, gs, gn, gb.reshape(hid)

    in_specs = (
        P("row", None), P(("row", "rep"), None, None), P(("row", "rep"), None),
        P(("row", "rep")), P(("row", "rep")), P(), P(), P(), P(("row", "rep"), None),
    )
    out_specs = (P(("row", "rep"), None), P(("row", "rep"), None), P(), P(), P())
    return jax.shard_map(
        per_device, mesh=mesh, in_specs=in_specs, out_specs=out_specs, check_vma=False)
```

```python
import jax
import jax.numpy as jnp
from jax import lax
from jax.experimental import pallas as pl
from jax.experimental.pallas import tpu as pltpu
from jax.sharding import PartitionSpec as P

MESH = pl.DeviceIdType.MESH
BF = jnp.bfloat16
F32 = jnp.float32


def swap_matrix(first, second):
    size = first * second
    out = lax.broadcasted_iota(jnp.int32, (size, size), 0)
    src = lax.broadcasted_iota(jnp.int32, (size, size), 1)
    match = (out // first == src % second) & (out % first == src // second)
    return match.astype(F32).astype(BF)


def dot(a, b):
    return jnp.dot(a, b, preferred_element_type=F32)


def make_kernel(nz, ny, nrep, tpd, blk, width, hid, nbd):
    cs = blk // nrep
    nodes = nbd * blk
    share = nodes // nrep
    half = nbd // 2
    npos = nbd * nz * ny
    hpos = npos // 2
    tiles_all = nrep * tpd
    scale = float(nz * ny * nodes) ** -0.5
    assert nz == ny == 8 and hid == 2 * width
    grows = 2 * width // ny
    F1N, F1F, F2, F3, B1N, B1F, GA, GB, GD = range(20, 38, 2)
    RL, F2N, F2F, RLN, RLF = range(40, 60, 4)
    GC = 13
    nx = nrep // 2

    def kernel(
        feat_in, tiles_in, owner, tblock, trow, w_self_in, w_neigh_in, bias_in, cot_in,
        hid_o, gf_o, gs_o, gn_o, gb_o,
        meta_s, meta, xt, ysend, tt, f2, turned, a0, a1, dense0, dense, dg0, dg, o0, b1, b2s, b2,
        ga0, ga, gb0, gb, gc0, gc, gd, relay3, relay4, kept,
        feat, tiles, w_self, w_neigh, bias, cot, load, send, recv,
    ):
        row = lax.axis_index("row")
        p = lax.axis_index("rep")
        z = row // ny
        y = row - z * ny

        def on_rep(q):
            return (row, q)

        def on_z(q):
            return (q * ny + y, p)

        def on_y(q):
            return (z * ny + q, p)

        axes = ((nrep, p, on_rep), (nz, z, on_z), (ny, y, on_y))
        rep_axis, z_axis, y_axis = axes

        def far_first(n):
            order = []
            for d in range(n // 2, 0, -1):
                order += [d] if n - d == d else [d, n - d]
            return order

        def others(axis):
            n, me, _ = axis
            if axis is rep_axis:
                x = me // 2
                core = me - 2 * x
                return [lax.rem(x + d, nx) * 2 + lax.rem(core + e, 2)
                        for d in far_first(nx) + [0] for e in (0, 1) if d or e]
            return [lax.rem(me + d, n) for d in far_first(n)]

        def seen(d):
            return (2 - d) % 8

        near, far = pl.ds(0, 5), pl.ds(5, 3)

        def off(axis, d):
            return lax.rem(axis[1] + (d + axis[0]), axis[0])

        def send_to(axis, t, src, dst, sem, left=None):
            pltpu.make_async_remote_copy(
                src_ref=src, dst_ref=dst, recv_sem=recv.at[sem],
                send_sem=send.at[sem if left is None else left],
                device_id=axis[2](t), device_id_type=MESH,
            ).start()

        def wait_bytes(ref, sem):
            pltpu.make_async_copy(ref, ref, sem).wait()

        def most(buf, n):
            return buf.at[pl.ds(0, n - 1)]

        barrier = pltpu.get_barrier_semaphore()
        count = 0
        for axis in (z_axis, y_axis, rep_axis):
            greeted = others(axis) if axis is rep_axis else [off(axis, d) for d in (2, -2, 1, -1)]
            for t in greeted:
                pl.semaphore_signal(barrier, inc=1, device_id=axis[2](t), device_id_type=MESH)
                count += 1

        loads = [
            pltpu.make_async_copy(src, dst, load.at[i]) for i, (src, dst) in enumerate((
                (feat_in, feat), (tiles_in, tiles), (w_self_in, w_self),
                (w_neigh_in, w_neigh), (bias_in, bias), (cot_in, cot)))]
        for copy in loads:
            copy.start()

        pl.semaphore_wait(barrier, count)

        loads[0].wait()
        start = pl.multiple_of(p * cs, cs)
        by_half = ((0, y_axis), (1, z_axis))
        by_other = ((0, z_axis), (1, y_axis))
        for d in (2, -2, 1, -1):
            for h, axis in by_other:
                send_to(axis, off(axis, d), feat.at[pl.ds(h * half, half), pl.ds(start, cs), :],
                        f2.at[h, 2, seen(d)], F1N + h)
        for h in range(2):
            f2[h, 2, 2] = feat[pl.ds(h * half, half), pl.ds(start, cs), :]

        lane = lax.broadcasted_iota(jnp.int32, (8, tiles_all), 1)
        code = jnp.zeros((8, tiles_all), jnp.int32)
        for k in range(tpd):
            own = owner[k]
            own_z = own // ny
            own_y = own - own_z * ny
            b = tblock[k]
            low = b - (b // half) * half
            rel_z, rel_y = lax.rem(own_z - z + nz + 2, nz), lax.rem(own_y - y + ny + 2, ny)
            first = rel_y * (2 * nz) + rel_z * half + low
            second = hpos + rel_z * (2 * ny) + rel_y * half + low
            where_to = jnp.where(b < half, first, second) + trow[k] * npos
            code = jnp.where(lane == p * tpd + k, where_to, code)
        meta_s[...] = code
        for t in others(rep_axis):
            send_to(rep_axis, t, meta_s, meta.at[p], 0)
        meta[p] = code

        loads[1].wait()
        for k in range(tpd):
            xt[k] = tiles[k].T
        tile_swap = swap_matrix(tpd, cs)

        def columns_of(t):
            part = xt[:, pl.ds(pl.multiple_of(t * cs, cs), cs), :].reshape(tpd * cs, blk)
            return dot(tile_swap, part).astype(BF).reshape(cs, tpd, blk)

        for t in others(rep_axis):
            ysend[t] = columns_of(t)
            send_to(rep_axis, t, ysend.at[t], tt.at[p], 1)
        tt[p] = columns_of(p)

        for batch, sem1, sem2, size in ((near, F1N, F2N, 4), (far, F1F, F2F, 3)):
            for h, axis in by_other:
                wait_bytes(f2.at[h, 2, pl.ds(0, size)], recv.at[sem1 + h])
                if sem1 != F1N:
                    continue
                for d in (2, -2):
                    got = f2.at[h, 2, 2 + d]
                    send_to(axis, off(axis, -d // 2), got, f2.at[h, 2, 5 if d > 0 else 7],
                            F1F + h, F1N + h)
                    part = pl.ds(half // 2 if d > 0 else 0, half // 2)
                    send_to(axis, off(axis, -d), got.at[part], f2.at[h, 2, 6, part],
                            F1F + h, F1N + h)
            for d in (2, -2, 1, -1):
                for h, axis in by_half:
                    sem = sem2 + 2 * h + (d < 0) if abs(d) == 2 else F2 + h
                    send_to(axis, off(axis, d), f2.at[h, 2, batch], f2.at[h, seen(d), batch],
                            sem, F2 + h)

        def pass_on(batch, sem2, parts):
            for d in (2, -2):
                for h, axis in by_half:
                    there = (2 + d) % 8
                    wait_bytes(f2.at[h, there, batch], recv.at[sem2 + 2 * h + (d > 0)])
                    send_to(axis, off(axis, -d // 2), f2.at[h, there, batch],
                            f2.at[h, 5 if d > 0 else 7, batch], F3 + h, F2 + h)
                    part = parts[d > 0]
                    send_to(axis, off(axis, -d), f2.at[h, there, part], f2.at[h, 6, part],
                            F3 + h, F2 + h)

        pass_on(near, F2N, (pl.ds(0, 3), pl.ds(3, 2)))

        wait_bytes(most(meta, nrep), recv.at[0])
        codes = meta[0]
        for q in range(1, nrep):
            codes = codes + meta[q]
        codes = codes[0:1, :]
        rows_of = codes // npos
        pos = codes - rows_of * npos
        wait_bytes(most(tt, nrep), recv.at[1])
        pos_iota = lax.broadcasted_iota(jnp.int32, (npos, tiles_all), 0)
        spread = jnp.concatenate(
            [(pos_iota + n * npos == codes).astype(F32).astype(BF) for n in range(nbd)], axis=0)
        for c in range(cs):
            placed = dot(spread, tt[:, c].reshape(tiles_all, blk)).astype(BF)
            for n in range(nbd):
                for h in range(2):
                    at = n * npos + h * hpos
                    dense0[h, :, c, :, n * blk:(n + 1) * blk] = placed[at:at + hpos].reshape(
                        ny, nz * half, blk)

        pass_on(far, F2F, (pl.ds(5, 1), pl.ds(6, 2)))
        chunk = nz * half * cs
        node_swap = swap_matrix(cs, nz * half)
        for h in range(2):
            for t in range(ny):
                piece = dot(node_swap, dense0[h, t].reshape(chunk, nodes)).astype(BF)
                dense[h, t] = piece
                at = (h * ny + t) * chunk
                turned[:, at:at + chunk] = piece.T

        for part, size, sem in ((slice(0, 5), 2, F2), (slice(5, 8), 3, F3)):
            for h in range(2):
                wait_bytes(f2.at[h, pl.ds(8 - size, size)], recv.at[sem + h])
                n = (part.stop - part.start) * chunk
                at = (h * ny + part.start) * chunk
                made = dot(turned[:, at:at + n], f2[h, part].reshape(n, width))
                partial = made if h == 0 and sem == F2 else partial + made
        a0[...] = partial.astype(BF).reshape(nrep, share, width)
        for t in others(rep_axis):
            send_to(rep_axis, t, a0.at[t], a1.at[p], 6)
        a1[p] = a0[p]

        for copy in loads[2:]:
            copy.wait()
        per_block = blk // share if share < blk else 1
        if share < blk:
            which = p // per_block
            inside = pl.multiple_of((p - which * per_block) * share, share)
            own = feat[which, pl.ds(inside, share), :]
        else:
            own = feat[pl.ds(p * (share // blk), share // blk)].reshape(share, width)
        own_part = dot(own, w_self[...]) + bias[...]

        wait_bytes(most(a1, nrep), recv.at[6])
        total = a1[0].astype(F32)
        for q in range(1, nrep):
            total = total + a1[q].astype(F32)
        agg = total.astype(BF)
        pre = own_part + dot(agg, w_neigh[...])
        sig = jax.nn.sigmoid(pre)
        dpre = cot[...].astype(F32) * sig * (1.0 + pre * (1.0 - sig))
        dpre_b = dpre.astype(BF)
        contract_cols = (((1,), (1,)), ((), ()))
        dagg = lax.dot_general(dpre_b, w_neigh[...], contract_cols, preferred_element_type=F32)
        dg0[...] = dagg.astype(BF)
        for t in others(rep_axis):
            send_to(rep_axis, t, dg0, dg.at[p], 7)
        dg[p] = dg0[...]
        hid_o[...] = (pre * sig).astype(BF)

        def summed(buf, n):
            acc = buf[0].astype(F32)
            for q in range(1, n):
                acc = acc + buf[q].astype(F32)
            return acc

        def two_parts(value):
            high = value.astype(BF).astype(F32)
            return jnp.concatenate([high, value - high], axis=0).astype(BF)

        contract_rows = (((0,), (0,)), ((), ()))
        bsum = jnp.sum(dpre, axis=0, keepdims=True)
        row8 = lax.broadcasted_iota(jnp.int32, (8, width), 0)
        bias_rows = two_parts(jnp.where(
            row8 == 0, bsum[:, :width], jnp.where(row8 == 1, bsum[:, width:], 0.0)))
        for h, left in ((0, own), (1, agg)):
            grads = lax.dot_general(left, dpre_b, contract_rows, preferred_element_type=F32)
            grads = jnp.concatenate([grads[:, :width], grads[:, width:]], axis=0).astype(BF)
            for q in range(ny):
                ga0[h, q, 0:grows, :] = grads[q * grows:(q + 1) * grows]
                if h == 0:
                    ga0[h, q, grows:, :] = bias_rows
        rows_in = (grows + 16, grows)
        for h, axis in by_half:
            for t in others(axis):
                send_to(axis, t, ga0.at[h, t, pl.ds(0, rows_in[h])],
                        ga.at[h, axis[1], pl.ds(0, rows_in[h])], GA + h)
            ga[h, axis[1]] = ga0[h, axis[1]]

        contract = lax.dot_general(dpre_b, w_self[...], contract_cols, preferred_element_type=F32)

        wait_bytes(most(dg, nrep), recv.at[7])
        dall = dg[...].reshape(nodes, width)

        def back_piece(h, t):
            return dot(dense[h, t], dall).reshape(nz, half * cs, width)

        def relay_four(sem, plus, minus):
            for h, axis in by_half:
                for d, part in ((2, plus), (-2, minus)):
                    send_to(axis, off(axis, d), o0.at[h, 6, part], relay4.at[h, part],
                            sem + 2 * h + (d < 0), RL + 2 + h)

        def relay_three(batch, sem):
            for h, axis in by_half:
                for d, t in ((1, 5), (-1, 7)):
                    send_to(axis, off(axis, d), o0.at[h, t, batch],
                            relay3.at[h, int(d < 0), batch], sem + 2 * h + (d < 0), RL + h)

        def next_out(batch, sem):
            for h, axis in by_half:
                for d, slot in ((1, 0), (-1, 1)):
                    send_to(axis, off(axis, d), o0.at[h, 2 + d, batch], b1.at[h, slot, batch],
                            sem + h, B1N + h)

        def make(*places):
            for t in places:
                for h in range(2):
                    o0[h, t] = back_piece(h, t).astype(BF)

        make(6)
        relay_four(RLF, pl.ds(5, 1), pl.ds(6, 2))
        make(5, 7)
        relay_three(far, RLF)
        relay_four(RLN, pl.ds(0, 3), pl.ds(3, 2))
        relay_three(near, RLN)
        make(1, 3)
        next_out(far, B1F)

        for h, axis in by_half:
            wait_bytes(ga.at[h, pl.ds(0, ny - 1), pl.ds(0, rows_in[h])], recv.at[GA + h])
            acc = summed(ga.at[h, :, pl.ds(0, rows_in[h])], ny)
            gb0[h, 0:grows] = acc[:grows].astype(BF)
            if h == 0:
                gb0[h, grows:] = two_parts(acc[grows:grows + 8] + acc[grows + 8:])
        for h, axis in by_other:
            for t in others(axis):
                send_to(axis, t, gb0.at[h, pl.ds(0, rows_in[h])],
                        gb.at[h, axis[1], pl.ds(0, rows_in[h])], GB + h)
            gb[h, axis[1]] = gb0[h]

        next_out(near, B1N)
        for h in range(2):
            kept[h, 0] = back_piece(h, 2)
            kept[h, 1] = back_piece(h, 4)
            kept[h, 2] = back_piece(h, 0)

        for lo, hi, sem, sem_out, cuts in ((5, 8, RLF, B1F, (6, 4, 5)), (0, 5, RLN, B1N, (3, 8, 7))):
            cut = cuts[0]
            for h, axis in by_half:
                for way, d in ((0, 2), (1, -2)):
                    wait_bytes(relay3.at[h, way, pl.ds(0, cuts[1 + way])],
                               recv.at[sem + 2 * h + way])
                    made = kept[h, 1 + way, lo:hi] + relay3[h, way, lo:hi].astype(F32)
                    first, second = made[:cut - lo], made[cut - lo:]
                    if way == 0:
                        first = first + relay4[h, lo:cut].astype(F32)
                    else:
                        second = second + relay4[h, cut:hi].astype(F32)
                    t = 2 + d
                    o0[h, t, lo:cut] = first.astype(BF)
                    o0[h, t, cut:hi] = second.astype(BF)
                    send_to(axis, off(axis, d), o0.at[h, t, pl.ds(lo, hi - lo)],
                            b1.at[h, 2 + way, pl.ds(lo, hi - lo)], sem_out + h, B1N + h)

        for h, axis in by_other:
            wait_bytes(gb.at[h, pl.ds(0, nz - 1), pl.ds(0, rows_in[h])], recv.at[GB + h])
            acc = summed(gb.at[h, :, pl.ds(0, rows_in[h])], nz)
            gc0[h * grows:(h + 1) * grows] = acc[:grows].astype(BF)
            if h == 0:
                gc0[2 * grows:] = two_parts(acc[grows:grows + 8] + acc[grows + 8:])
        for t in others(rep_axis):
            send_to(rep_axis, t, gc0, gc.at[p], GC)
        gc[p] = gc0[...]

        for lo, hi, sem, order in ((5, 8, B1F, (4, 3, -3)), (0, 5, B1N, (2, -2, 1, -1, 0))):
            for h, axis in by_other:
                wait_bytes(b1.at[h, :, pl.ds(lo, hi - lo)], recv.at[sem + h])
                acc = kept[h, 0, lo:hi]
                for q in range(4):
                    acc = acc + b1[h, q, lo:hi].astype(F32)
                b2s[h, lo:hi] = acc.astype(BF).reshape(hi - lo, half, cs, width)
                for d in order:
                    for low in range(half):
                        b = h * half + low
                        node = b * blk + p * cs
                        to = node // share
                        into = b2.at[seen(d), (node - to * share) // cs]
                        mine = b2s.at[h, (2 + d) % 8, low]
                        if d != 0:
                            t = off(axis, d)
                            place = (t * ny + y, to) if h == 0 else (z * ny + t, to)
                            pltpu.make_async_remote_copy(
                                src_ref=mine, dst_ref=into, send_sem=send.at[10],
                                recv_sem=recv.at[10], device_id=place, device_id_type=MESH,
                            ).start()
                            continue

                        @pl.when(to == p)
                        def _():
                            pltpu.make_async_copy(mine, into, recv.at[10]).start()

                        @pl.when(to != p)
                        def _():
                            send_to(rep_axis, to, mine, into, 10, 14 + b)

        wait_bytes(most(gc, nrep), recv.at[GC])
        acc = summed(gc, nrep) * scale
        gbias = acc[2 * grows:2 * grows + 8] + acc[2 * grows + 8:]
        gb_o[...] = jnp.concatenate([gbias[0:1], gbias[1:2]], axis=1)
        for h, axis in by_half:
            me = axis[1]
            gd[h, me] = acc[h * grows:(h + 1) * grows].astype(BF)
            for t in others(axis):
                send_to(axis, t, gd.at[h, me], gd.at[h, me], GD + h)

        wait_bytes(b2, recv.at[10])
        gf_o[...] = contract + summed(b2, nz).reshape(share, width)
        for h, out in ((0, gs_o), (1, gn_o)):
            wait_bytes(most(gd.at[h], ny), recv.at[GD + h])
            every = gd[h].reshape(2, width, width).astype(F32)
            for c in range(2):
                out[:, c * width:(c + 1) * width] = every[c]

        wait_bytes(most(meta, nrep), send.at[0])
        wait_bytes(most(tt, nrep), send.at[1])
        for h in range(2):
            wait_bytes(f2.at[h, 2, pl.ds(0, 7)], send.at[F1N + h])
            wait_bytes(f2.at[h, pl.ds(0, 7)], send.at[F2 + h])
            wait_bytes(relay3.at[h], send.at[RL + h])
            wait_bytes(relay4.at[h], send.at[RL + 2 + h])
            wait_bytes(b1.at[h], send.at[B1N + h])
            wait_bytes(ga.at[h, pl.ds(0, ny - 1), pl.ds(0, rows_in[h])], send.at[GA + h])
            wait_bytes(gb.at[h, pl.ds(0, nz - 1), pl.ds(0, rows_in[h])], send.at[GB + h])
            wait_bytes(most(gd.at[h], ny), send.at[GD + h])
        wait_bytes(most(a1, nrep), send.at[6])
        wait_bytes(most(dg, nrep), send.at[7])
        wait_bytes(most(b2, nz), send.at[10])
        for b in range(nbd):
            node = b * blk + p * cs

            @pl.when(node // share != p)
            def _():
                wait_bytes(b2s.at[0, 0, 0], send.at[14 + b])
        wait_bytes(most(gc, nrep), send.at[GC])

    V = pltpu.VMEM
    scratch = [
        V((8, tiles_all), jnp.int32),
        V((nrep, 8, tiles_all), jnp.int32),
        V((tpd, blk, blk), BF),
        V((nrep, cs, tpd, blk), BF),
        V((nrep, cs, tpd, blk), BF),
        V((2, ny, nz, half, cs, width), BF),
        V((nodes, npos * cs), BF),
        V((nrep, share, width), BF),
        V((nrep, share, width), BF),
        V((2, ny, cs, nz * half, nodes), BF),
        V((2, ny, nz * half * cs, nodes), BF),
        V((share, width), BF),
        V((nrep, share, width), BF),
        V((2, ny, nz, half * cs, width), BF),
        V((2, 4, nz, half * cs, width), BF),
        V((2, nz, half, cs, width), BF),
        V((nz, share // cs, cs, width), BF),
        V((2, ny, grows + 16, width), BF),
        V((2, ny, grows + 16, width), BF),
        V((2, grows + 16, width), BF),
        V((2, nz, grows + 16, width), BF),
        V((2 * grows + 16, width), BF),
        V((nrep, 2 * grows + 16, width), BF),
        V((2, ny, grows, width), BF),
        V((2, 2, nz, half * cs, width), BF),
        V((2, nz, half * cs, width), BF),
        V((2, 3, nz, half * cs, width), F32),
        V((nbd, blk, width), BF),
        V((tpd, blk, blk), BF),
        V((width, hid), BF),
        V((width, hid), BF),
        V((1, hid), F32),
        V((share, hid), BF),
        pltpu.SemaphoreType.DMA((6,)),
        pltpu.SemaphoreType.DMA((60,)),
        pltpu.SemaphoreType.DMA((60,)),
    ]
    outs = (
        jax.ShapeDtypeStruct((share, hid), BF),
        jax.ShapeDtypeStruct((share, width), F32),
        jax.ShapeDtypeStruct((width, hid), F32),
        jax.ShapeDtypeStruct((width, hid), F32),
        jax.ShapeDtypeStruct((1, hid), F32),
    )
    vmem, smem = pl.BlockSpec(memory_space=pltpu.VMEM), pl.BlockSpec(memory_space=pltpu.SMEM)
    there = pl.BlockSpec(memory_space=pl.ANY)
    return pl.pallas_call(
        kernel,
        out_shape=outs,
        in_specs=[there, there, smem, smem, smem, there, there, there, there],
        out_specs=tuple([vmem] * 5),
        scratch_shapes=scratch,
        compiler_params=pltpu.CompilerParams(
            collective_id=0, has_side_effects=True, vmem_limit_bytes=56 * 1024 * 1024),
    )


def finish(results):
    def kernel(*refs):
        n = len(results)
        copies = [pltpu.make_async_copy(refs[i], refs[n + i], refs[2 * n].at[i]) for i in range(n)]
        for copy in copies:
            copy.start()
        for copy in copies:
            copy.wait()

    anywhere = pl.BlockSpec(memory_space=pl.ANY)
    return pl.pallas_call(
        kernel,
        out_shape=tuple(jax.ShapeDtypeStruct(r.shape, r.dtype) for r in results),
        in_specs=[pl.BlockSpec(memory_space=pltpu.VMEM)] * len(results),
        out_specs=tuple([anywhere] * len(results)),
        scratch_shapes=[pltpu.SemaphoreType.DMA((len(results),))],
    )(*results)


def solution(mesh):
    nrow, nrep = mesh.shape["row"], mesh.shape["rep"]
    side = int(round(nrow ** 0.5))

    def per_device(features, edge_tiles, tile_owner, tile_block, tile_row, w_self, w_neigh,
                   bias_vector, cotangent):
        tpd, blk, _ = edge_tiles.shape
        nodes, width = features.shape
        hid = w_self.shape[1]
        nbd = nodes // blk
        call = make_kernel(side, nrow // side, nrep, tpd, blk, width, hid, nbd)
        results = call(
            features.reshape(nbd, blk, width), edge_tiles, tile_owner.reshape(tpd), tile_block, tile_row,
            w_self, w_neigh, bias_vector.reshape(1, hid), cotangent)
        hidden, gf, gs, gn, gb = finish(results)
        return hidden, gf, gs, gn, gb.reshape(hid)

    in_specs = (
        P("row", None), P(("row", "rep"), None, None), P(("row", "rep"), None),
        P(("row", "rep")), P(("row", "rep")), P(), P(), P(), P(("row", "rep"), None),
    )
    out_specs = (P(("row", "rep"), None), P(("row", "rep"), None), P(), P(), P())
    return jax.shard_map(
        per_device, mesh=mesh, in_specs=in_specs, out_specs=out_specs, check_vma=False)
```

```python
import jax
import jax.numpy as jnp
from jax import lax
from jax.experimental import pallas as pl
from jax.experimental.pallas import tpu as pltpu
from jax.sharding import PartitionSpec as P

MESH = pl.DeviceIdType.MESH
BF = jnp.bfloat16
F32 = jnp.float32


def swap_matrix(first, second):
    size = first * second
    out = lax.broadcasted_iota(jnp.int32, (size, size), 0)
    src = lax.broadcasted_iota(jnp.int32, (size, size), 1)
    match = (out // first == src % second) & (out % first == src // second)
    return match.astype(F32).astype(BF)


def dot(a, b):
    return jnp.dot(a, b, preferred_element_type=F32)


def make_kernel(nz, ny, nrep, tpd, blk, width, hid, nbd):
    cs = blk // nrep
    nodes = nbd * blk
    share = nodes // nrep
    half = nbd // 2
    npos = nbd * nz * ny
    hpos = npos // 2
    tiles_all = nrep * tpd
    scale = float(nz * ny * nodes) ** -0.5
    assert nz == ny == 8 and hid == 2 * width
    grows = 2 * width // ny
    F1N, F1F, F2, F3, B1N, B1F, GA, GB, GD = range(20, 38, 2)
    RL, F2N, F2F, RLN, RLF = range(40, 60, 4)
    GC = 13
    nx = nrep // 2

    def kernel(
        feat_in, tiles_in, owner, tblock, trow, w_self_in, w_neigh_in, bias_in, cot_in,
        hid_o, gf_o, gs_o, gn_o, gb_o,
        meta_s, meta, xt, ysend, tt, f2, turned, a0, a1, dense0, dense, dg0, dg, o0, b1, b2s, b2,
        ga0, ga, gb0, gb, gc0, gc, gd, relay3, relay4, kept,
        feat, tiles, w_self, w_neigh, bias, cot, load, send, recv,
    ):
        row = lax.axis_index("row")
        p = lax.axis_index("rep")
        z = row // ny
        y = row - z * ny

        def on_rep(q):
            return (row, q)

        def on_z(q):
            return (q * ny + y, p)

        def on_y(q):
            return (z * ny + q, p)

        axes = ((nrep, p, on_rep), (nz, z, on_z), (ny, y, on_y))
        rep_axis, z_axis, y_axis = axes

        def far_first(n):
            order = []
            for d in range(n // 2, 0, -1):
                order += [d] if n - d == d else [d, n - d]
            return order

        def others(axis):
            n, me, _ = axis
            if axis is rep_axis:
                x = me // 2
                core = me - 2 * x
                return [lax.rem(x + d, nx) * 2 + lax.rem(core + e, 2)
                        for d in far_first(nx) + [0] for e in (0, 1) if d or e]
            return [lax.rem(me + d, n) for d in far_first(n)]

        def seen(d):
            return (2 - d) % 8

        near, far = pl.ds(0, 5), pl.ds(5, 3)

        def off(axis, d):
            return lax.rem(axis[1] + (d + axis[0]), axis[0])

        def send_to(axis, t, src, dst, sem, left=None):
            pltpu.make_async_remote_copy(
                src_ref=src, dst_ref=dst, recv_sem=recv.at[sem],
                send_sem=send.at[sem if left is None else left],
                device_id=axis[2](t), device_id_type=MESH,
            ).start()

        def wait_bytes(ref, sem):
            pltpu.make_async_copy(ref, ref, sem).wait()

        def most(buf, n):
            return buf.at[pl.ds(0, n - 1)]

        barrier = pltpu.get_barrier_semaphore()
        count = 0
        for axis in (z_axis, y_axis, rep_axis):
            greeted = others(axis) if axis is rep_axis else [off(axis, d) for d in (2, -2, 1, -1)]
            for t in greeted:
                pl.semaphore_signal(barrier, inc=1, device_id=axis[2](t), device_id_type=MESH)
                count += 1

        loads = [
            pltpu.make_async_copy(src, dst, load.at[i]) for i, (src, dst) in enumerate((
                (feat_in, feat), (tiles_in, tiles), (w_self_in, w_self),
                (w_neigh_in, w_neigh), (bias_in, bias), (cot_in, cot)))]
        for copy in loads:
            copy.start()

        pl.semaphore_wait(barrier, count)

        loads[0].wait()
        start = pl.multiple_of(p * cs, cs)
        by_half = ((0, y_axis), (1, z_axis))
        by_other = ((0, z_axis), (1, y_axis))
        for d in (2, -2, 1, -1):
            for h, axis in by_other:
                send_to(axis, off(axis, d), feat.at[pl.ds(h * half, half), pl.ds(start, cs), :],
                        f2.at[h, 2, seen(d)], F1N + h)
        for h in range(2):
            f2[h, 2, 2] = feat[pl.ds(h * half, half), pl.ds(start, cs), :]

        lane = lax.broadcasted_iota(jnp.int32, (8, tiles_all), 1)
        code = jnp.zeros((8, tiles_all), jnp.int32)
        for k in range(tpd):
            own = owner[k]
            own_z = own // ny
            own_y = own - own_z * ny
            b = tblock[k]
            low = b - (b // half) * half
            rel_z, rel_y = lax.rem(own_z - z + nz + 2, nz), lax.rem(own_y - y + ny + 2, ny)
            first = rel_y * (2 * nz) + rel_z * half + low
            second = hpos + rel_z * (2 * ny) + rel_y * half + low
            where_to = jnp.where(b < half, first, second) + trow[k] * npos
            code = jnp.where(lane == p * tpd + k, where_to, code)
        meta_s[...] = code
        for t in others(rep_axis):
            send_to(rep_axis, t, meta_s, meta.at[p], 0)
        meta[p] = code

        loads[1].wait()
        for k in range(tpd):
            xt[k] = tiles[k].T
        tile_swap = swap_matrix(tpd, cs)

        def columns_of(t):
            part = xt[:, pl.ds(pl.multiple_of(t * cs, cs), cs), :].reshape(tpd * cs, blk)
            return dot(tile_swap, part).astype(BF).reshape(cs, tpd, blk)

        for t in others(rep_axis):
            ysend[t] = columns_of(t)
            send_to(rep_axis, t, ysend.at[t], tt.at[p], 1)
        tt[p] = columns_of(p)

        for batch, sem1, sem2, size in ((near, F1N, F2N, 4), (far, F1F, F2F, 3)):
            for h, axis in by_other:
                wait_bytes(f2.at[h, 2, pl.ds(0, size)], recv.at[sem1 + h])
                if sem1 != F1N:
                    continue
                for d in (2, -2):
                    got = f2.at[h, 2, 2 + d]
                    send_to(axis, off(axis, -d // 2), got, f2.at[h, 2, 5 if d > 0 else 7],
                            F1F + h, F1N + h)
                    part = pl.ds(half // 2 if d > 0 else 0, half // 2)
                    send_to(axis, off(axis, -d), got.at[part], f2.at[h, 2, 6, part],
                            F1F + h, F1N + h)
            for d in (2, -2, 1, -1):
                for h, axis in by_half:
                    sem = sem2 + 2 * h + (d < 0) if abs(d) == 2 else F2 + h
                    send_to(axis, off(axis, d), f2.at[h, 2, batch], f2.at[h, seen(d), batch],
                            sem, F2 + h)

        def pass_on(batch, sem2, parts):
            for d in (2, -2):
                for h, axis in by_half:
                    there = (2 + d) % 8
                    wait_bytes(f2.at[h, there, batch], recv.at[sem2 + 2 * h + (d > 0)])
                    send_to(axis, off(axis, -d // 2), f2.at[h, there, batch],
                            f2.at[h, 5 if d > 0 else 7, batch], F3 + h, F2 + h)
                    part = parts[d > 0]
                    send_to(axis, off(axis, -d), f2.at[h, there, part], f2.at[h, 6, part],
                            F3 + h, F2 + h)

        pass_on(near, F2N, (pl.ds(0, 3), pl.ds(3, 2)))
        pass_on(far, F2F, (pl.ds(5, 1), pl.ds(6, 2)))

        wait_bytes(most(meta, nrep), recv.at[0])
        codes = meta[0]
        for q in range(1, nrep):
            codes = codes + meta[q]
        codes = codes[0:1, :]
        rows_of = codes // npos
        pos = codes - rows_of * npos
        wait_bytes(most(tt, nrep), recv.at[1])
        pos_iota = lax.broadcasted_iota(jnp.int32, (npos, tiles_all), 0)
        spread = jnp.concatenate(
            [(pos_iota + n * npos == codes).astype(F32).astype(BF) for n in range(nbd)], axis=0)
        for c in range(cs):
            placed = dot(spread, tt[:, c].reshape(tiles_all, blk)).astype(BF)
            for n in range(nbd):
                for h in range(2):
                    at = n * npos + h * hpos
                    dense0[h, :, c, :, n * blk:(n + 1) * blk] = placed[at:at + hpos].reshape(
                        ny, nz * half, blk)

        chunk = nz * half * cs
        node_swap = swap_matrix(cs, nz * half)
        for h in range(2):
            for t in range(ny):
                piece = dot(node_swap, dense0[h, t].reshape(chunk, nodes)).astype(BF)
                dense[h, t] = piece
                at = (h * ny + t) * chunk
                turned[:, at:at + chunk] = piece.T

        for part, size, sem in ((slice(0, 5), 2, F2), (slice(5, 8), 3, F3)):
            for h in range(2):
                wait_bytes(f2.at[h, pl.ds(8 - size, size)], recv.at[sem + h])
                n = (part.stop - part.start) * chunk
                at = (h * ny + part.start) * chunk
                made = dot(turned[:, at:at + n], f2[h, part].reshape(n, width))
                partial = made if h == 0 and sem == F2 else partial + made
        a0[...] = partial.astype(BF).reshape(nrep, share, width)
        for t in others(rep_axis):
            send_to(rep_axis, t, a0.at[t], a1.at[p], 6)
        a1[p] = a0[p]

        for copy in loads[2:]:
            copy.wait()
        per_block = blk // share if share < blk else 1
        if share < blk:
            which = p // per_block
            inside = pl.multiple_of((p - which * per_block) * share, share)
            own = feat[which, pl.ds(inside, share), :]
        else:
            own = feat[pl.ds(p * (share // blk), share // blk)].reshape(share, width)
        own_part = dot(own, w_self[...]) + bias[...]

        wait_bytes(most(a1, nrep), recv.at[6])
        total = a1[0].astype(F32)
        for q in range(1, nrep):
            total = total + a1[q].astype(F32)
        agg = total.astype(BF)
        pre = own_part + dot(agg, w_neigh[...])
        sig = jax.nn.sigmoid(pre)
        dpre = cot[...].astype(F32) * sig * (1.0 + pre * (1.0 - sig))
        dpre_b = dpre.astype(BF)
        contract_cols = (((1,), (1,)), ((), ()))
        dagg = lax.dot_general(dpre_b, w_neigh[...], contract_cols, preferred_element_type=F32)
        dg0[...] = dagg.astype(BF)
        for t in others(rep_axis):
            send_to(rep_axis, t, dg0, dg.at[p], 7)
        dg[p] = dg0[...]
        hid_o[...] = (pre * sig).astype(BF)

        def summed(buf, n):
            acc = buf[0].astype(F32)
            for q in range(1, n):
                acc = acc + buf[q].astype(F32)
            return acc

        def two_parts(value):
            high = value.astype(BF).astype(F32)
            return jnp.concatenate([high, value - high], axis=0).astype(BF)

        contract_rows = (((0,), (0,)), ((), ()))
        bsum = jnp.sum(dpre, axis=0, keepdims=True)
        row8 = lax.broadcasted_iota(jnp.int32, (8, width), 0)
        bias_rows = two_parts(jnp.where(
            row8 == 0, bsum[:, :width], jnp.where(row8 == 1, bsum[:, width:], 0.0)))
        for h, left in ((0, own), (1, agg)):
            grads = lax.dot_general(left, dpre_b, contract_rows, preferred_element_type=F32)
            grads = jnp.concatenate([grads[:, :width], grads[:, width:]], axis=0).astype(BF)
            for q in range(ny):
                ga0[h, q, 0:grows, :] = grads[q * grows:(q + 1) * grows]
                if h == 0:
                    ga0[h, q, grows:, :] = bias_rows
        rows_in = (grows + 16, grows)
        for h, axis in by_half:
            for t in others(axis):
                send_to(axis, t, ga0.at[h, t, pl.ds(0, rows_in[h])],
                        ga.at[h, axis[1], pl.ds(0, rows_in[h])], GA + h)
            ga[h, axis[1]] = ga0[h, axis[1]]

        contract = lax.dot_general(dpre_b, w_self[...], contract_cols, preferred_element_type=F32)

        wait_bytes(most(dg, nrep), recv.at[7])
        dall = dg[...].reshape(nodes, width)

        def back_piece(h, t):
            return dot(dense[h, t], dall).reshape(nz, half * cs, width)

        def relay_four(sem, plus, minus):
            for h, axis in by_half:
                for d, part in ((2, plus), (-2, minus)):
                    send_to(axis, off(axis, d), o0.at[h, 6, part], relay4.at[h, part],
                            sem + 2 * h + (d < 0), RL + 2 + h)

        def relay_three(batch, sem):
            for h, axis in by_half:
                for d, t in ((1, 5), (-1, 7)):
                    send_to(axis, off(axis, d), o0.at[h, t, batch],
                            relay3.at[h, int(d < 0), batch], sem + 2 * h + (d < 0), RL + h)

        def next_out(batch, sem):
            for h, axis in by_half:
                for d, slot in ((1, 0), (-1, 1)):
                    send_to(axis, off(axis, d), o0.at[h, 2 + d, batch], b1.at[h, slot, batch],
                            sem + h, B1N + h)

        def make(*places):
            for t in places:
                for h in range(2):
                    o0[h, t] = back_piece(h, t).astype(BF)

        make(6)
        relay_four(RLF, pl.ds(5, 1), pl.ds(6, 2))
        make(5, 7)
        relay_three(far, RLF)
        relay_four(RLN, pl.ds(0, 3), pl.ds(3, 2))
        relay_three(near, RLN)
        make(1, 3)
        next_out(far, B1F)

        for h, axis in by_half:
            wait_bytes(ga.at[h, pl.ds(0, ny - 1), pl.ds(0, rows_in[h])], recv.at[GA + h])
            acc = summed(ga.at[h, :, pl.ds(0, rows_in[h])], ny)
            gb0[h, 0:grows] = acc[:grows].astype(BF)
            if h == 0:
                gb0[h, grows:] = two_parts(acc[grows:grows + 8] + acc[grows + 8:])
        for h, axis in by_other:
            for t in others(axis):
                send_to(axis, t, gb0.at[h, pl.ds(0, rows_in[h])],
                        gb.at[h, axis[1], pl.ds(0, rows_in[h])], GB + h)
            gb[h, axis[1]] = gb0[h]

        next_out(near, B1N)
        for h in range(2):
            kept[h, 0] = back_piece(h, 2)
            kept[h, 1] = back_piece(h, 4)
            kept[h, 2] = back_piece(h, 0)

        for lo, hi, sem, sem_out, cuts in ((5, 8, RLF, B1F, (6, 4, 5)), (0, 5, RLN, B1N, (3, 8, 7))):
            cut = cuts[0]
            for h, axis in by_half:
                for way, d in ((0, 2), (1, -2)):
                    wait_bytes(relay3.at[h, way, pl.ds(0, cuts[1 + way])],
                               recv.at[sem + 2 * h + way])
                    made = kept[h, 1 + way, lo:hi] + relay3[h, way, lo:hi].astype(F32)
                    first, second = made[:cut - lo], made[cut - lo:]
                    if way == 0:
                        first = first + relay4[h, lo:cut].astype(F32)
                    else:
                        second = second + relay4[h, cut:hi].astype(F32)
                    t = 2 + d
                    o0[h, t, lo:cut] = first.astype(BF)
                    o0[h, t, cut:hi] = second.astype(BF)
                    send_to(axis, off(axis, d), o0.at[h, t, pl.ds(lo, hi - lo)],
                            b1.at[h, 2 + way, pl.ds(lo, hi - lo)], sem_out + h, B1N + h)

        for h, axis in by_other:
            wait_bytes(gb.at[h, pl.ds(0, nz - 1), pl.ds(0, rows_in[h])], recv.at[GB + h])
            acc = summed(gb.at[h, :, pl.ds(0, rows_in[h])], nz)
            gc0[h * grows:(h + 1) * grows] = acc[:grows].astype(BF)
            if h == 0:
                gc0[2 * grows:] = two_parts(acc[grows:grows + 8] + acc[grows + 8:])
        for t in others(rep_axis):
            send_to(rep_axis, t, gc0, gc.at[p], GC)
        gc[p] = gc0[...]

        for lo, hi, sem, order in ((5, 8, B1F, (4, 3, -3)), (0, 5, B1N, (2, -2, 1, -1, 0))):
            for h, axis in by_other:
                wait_bytes(b1.at[h, :, pl.ds(lo, hi - lo)], recv.at[sem + h])
                acc = kept[h, 0, lo:hi]
                for q in range(4):
                    acc = acc + b1[h, q, lo:hi].astype(F32)
                b2s[h, lo:hi] = acc.astype(BF).reshape(hi - lo, half, cs, width)
                for d in order:
                    for low in range(half):
                        b = h * half + low
                        node = b * blk + p * cs
                        to = node // share
                        into = b2.at[seen(d), (node - to * share) // cs]
                        mine = b2s.at[h, (2 + d) % 8, low]
                        if d != 0:
                            t = off(axis, d)
                            place = (t * ny + y, to) if h == 0 else (z * ny + t, to)
                            pltpu.make_async_remote_copy(
                                src_ref=mine, dst_ref=into, send_sem=send.at[10],
                                recv_sem=recv.at[10], device_id=place, device_id_type=MESH,
                            ).start()
                            continue

                        @pl.when(to == p)
                        def _():
                            pltpu.make_async_copy(mine, into, recv.at[10]).start()

                        @pl.when(to != p)
                        def _():
                            send_to(rep_axis, to, mine, into, 10, 14 + b)

        wait_bytes(most(gc, nrep), recv.at[GC])
        acc = summed(gc, nrep) * scale
        gbias = acc[2 * grows:2 * grows + 8] + acc[2 * grows + 8:]
        gb_o[...] = jnp.concatenate([gbias[0:1], gbias[1:2]], axis=1)
        for h, axis in by_half:
            me = axis[1]
            gd[h, me] = acc[h * grows:(h + 1) * grows].astype(BF)
            for t in others(axis):
                send_to(axis, t, gd.at[h, me], gd.at[h, me], GD + h)

        wait_bytes(b2, recv.at[10])
        gf_o[...] = contract + summed(b2, nz).reshape(share, width)
        for h, out in ((0, gs_o), (1, gn_o)):
            wait_bytes(most(gd.at[h], ny), recv.at[GD + h])
            every = gd[h].reshape(2, width, width).astype(F32)
            for c in range(2):
                out[:, c * width:(c + 1) * width] = every[c]

        wait_bytes(most(meta, nrep), send.at[0])
        wait_bytes(most(tt, nrep), send.at[1])
        for h in range(2):
            wait_bytes(f2.at[h, 2, pl.ds(0, 7)], send.at[F1N + h])
            wait_bytes(f2.at[h, pl.ds(0, 7)], send.at[F2 + h])
            wait_bytes(relay3.at[h], send.at[RL + h])
            wait_bytes(relay4.at[h], send.at[RL + 2 + h])
            wait_bytes(b1.at[h], send.at[B1N + h])
            wait_bytes(ga.at[h, pl.ds(0, ny - 1), pl.ds(0, rows_in[h])], send.at[GA + h])
            wait_bytes(gb.at[h, pl.ds(0, nz - 1), pl.ds(0, rows_in[h])], send.at[GB + h])
            wait_bytes(most(gd.at[h], ny), send.at[GD + h])
        wait_bytes(most(a1, nrep), send.at[6])
        wait_bytes(most(dg, nrep), send.at[7])
        wait_bytes(most(b2, nz), send.at[10])
        for b in range(nbd):
            node = b * blk + p * cs

            @pl.when(node // share != p)
            def _():
                wait_bytes(b2s.at[0, 0, 0], send.at[14 + b])
        wait_bytes(most(gc, nrep), send.at[GC])

    V = pltpu.VMEM
    scratch = [
        V((8, tiles_all), jnp.int32),
        V((nrep, 8, tiles_all), jnp.int32),
        V((tpd, blk, blk), BF),
        V((nrep, cs, tpd, blk), BF),
        V((nrep, cs, tpd, blk), BF),
        V((2, ny, nz, half, cs, width), BF),
        V((nodes, npos * cs), BF),
        V((nrep, share, width), BF),
        V((nrep, share, width), BF),
        V((2, ny, cs, nz * half, nodes), BF),
        V((2, ny, nz * half * cs, nodes), BF),
        V((share, width), BF),
        V((nrep, share, width), BF),
        V((2, ny, nz, half * cs, width), BF),
        V((2, 4, nz, half * cs, width), BF),
        V((2, nz, half, cs, width), BF),
        V((nz, share // cs, cs, width), BF),
        V((2, ny, grows + 16, width), BF),
        V((2, ny, grows + 16, width), BF),
        V((2, grows + 16, width), BF),
        V((2, nz, grows + 16, width), BF),
        V((2 * grows + 16, width), BF),
        V((nrep, 2 * grows + 16, width), BF),
        V((2, ny, grows, width), BF),
        V((2, 2, nz, half * cs, width), BF),
        V((2, nz, half * cs, width), BF),
        V((2, 3, nz, half * cs, width), F32),
        V((nbd, blk, width), BF),
        V((tpd, blk, blk), BF),
        V((width, hid), BF),
        V((width, hid), BF),
        V((1, hid), F32),
        V((share, hid), BF),
        pltpu.SemaphoreType.DMA((6,)),
        pltpu.SemaphoreType.DMA((60,)),
        pltpu.SemaphoreType.DMA((60,)),
    ]
    outs = (
        jax.ShapeDtypeStruct((share, hid), BF),
        jax.ShapeDtypeStruct((share, width), F32),
        jax.ShapeDtypeStruct((width, hid), F32),
        jax.ShapeDtypeStruct((width, hid), F32),
        jax.ShapeDtypeStruct((1, hid), F32),
    )
    vmem, smem = pl.BlockSpec(memory_space=pltpu.VMEM), pl.BlockSpec(memory_space=pltpu.SMEM)
    there = pl.BlockSpec(memory_space=pl.ANY)
    return pl.pallas_call(
        kernel,
        out_shape=outs,
        in_specs=[there, there, smem, smem, smem, there, there, there, there],
        out_specs=tuple([vmem] * 5),
        scratch_shapes=scratch,
        compiler_params=pltpu.CompilerParams(
            collective_id=0, has_side_effects=True, vmem_limit_bytes=56 * 1024 * 1024),
    )


def finish(results):
    def kernel(*refs):
        n = len(results)
        copies = [pltpu.make_async_copy(refs[i], refs[n + i], refs[2 * n].at[i]) for i in range(n)]
        for copy in copies:
            copy.start()
        for copy in copies:
            copy.wait()

    anywhere = pl.BlockSpec(memory_space=pl.ANY)
    return pl.pallas_call(
        kernel,
        out_shape=tuple(jax.ShapeDtypeStruct(r.shape, r.dtype) for r in results),
        in_specs=[pl.BlockSpec(memory_space=pltpu.VMEM)] * len(results),
        out_specs=tuple([anywhere] * len(results)),
        scratch_shapes=[pltpu.SemaphoreType.DMA((len(results),))],
    )(*results)


def solution(mesh):
    nrow, nrep = mesh.shape["row"], mesh.shape["rep"]
    side = int(round(nrow ** 0.5))

    def per_device(features, edge_tiles, tile_owner, tile_block, tile_row, w_self, w_neigh,
                   bias_vector, cotangent):
        tpd, blk, _ = edge_tiles.shape
        nodes, width = features.shape
        hid = w_self.shape[1]
        nbd = nodes // blk
        call = make_kernel(side, nrow // side, nrep, tpd, blk, width, hid, nbd)
        results = call(
            features.reshape(nbd, blk, width), edge_tiles, tile_owner.reshape(tpd), tile_block, tile_row,
            w_self, w_neigh, bias_vector.reshape(1, hid), cotangent)
        hidden, gf, gs, gn, gb = finish(results)
        return hidden, gf, gs, gn, gb.reshape(hid)

    in_specs = (
        P("row", None), P(("row", "rep"), None, None), P(("row", "rep"), None),
        P(("row", "rep")), P(("row", "rep")), P(), P(), P(), P(("row", "rep"), None),
    )
    out_specs = (P(("row", "rep"), None), P(("row", "rep"), None), P(), P(), P())
    return jax.shard_map(
        per_device, mesh=mesh, in_specs=in_specs, out_specs=out_specs, check_vma=False)
```
